32 devices in a mesh: grp: 2 (over core), ep: 16 (over z, y, x).
Axes of the slice: x: 2, y: 2, z: 4, core: 2. Of those that a mesh axis runs over, the one named last changes fastest.
Arguments:
- tokens: bfloat16 [2, 2048, 1024], P('grp', 'ep'), may hold values from -6 to 6
- queries: bfloat16 [2, 2048, 1024], P('grp', 'ep'), may hold values from -128 to 128
- keys: bfloat16 [2, 2048, 1024], P('grp', 'ep'), may hold values from -4 to 4
- values: bfloat16 [2, 2048, 1024], P('grp', 'ep'), may hold values from -6 to 6
- key_mask: int32 [2, 2048], P('grp', 'ep'), may hold values 0 or 1
- labels: int32 [2, 2048, 1], P('grp', 'ep'), may hold values from 0 to 3; in each aligned block of 128 rows (0 to 127, 128 to 255, ..., all dimensions but the last counted through in order) at most 36 rows name the same one
- cotangent: bfloat16 [2, 2048, 1024], P('grp', 'ep'), may hold values from -0.125 to 0.125
- weight_in: bfloat16 [1024, 16384], P(None, 'ep'), may hold values from -0.1875 to 0.1875
- weight_out: bfloat16 [16, 1024, 1024], P('ep'), may hold values from -0.09375 to 0.09375
Outputs:
- layer_out: bfloat16 [2, 2048, 1024], P('grp', 'ep')
- grad_out: bfloat16 [16, 1024, 1024], P('ep', 'grp')
The draws below stay inside these ranges and needn't reach their ends.
Inputs may be any that keep to these rules, and one draw needn't show every extreme that they name: `labels`: among the 128 tokens of one aligned block of a sample no label occurs more than 36 times, and some block reaches 36.
All inputs are finite; a program needn't handle non-finite values. No bound on the sum of `key_mask` on one device may be relied on, other than what follows from the above.
Results may differ from the reference program's by a relative error of at most 0.018.
Values may be sent and summed in bfloat16 or wider, within the bound.
No kernel may reach another device: no remote copies, remote signals or barrier semaphores. Data moves between devices by JAX's collectives and lax.ppermute only.
A program may use at most 64 MiB of HBM per device.

```python
import math
import jax
import jax.numpy as jnp
import numpy as np
from jax import lax

D = 1024
FF = 4096
HEADS = 8
SPLIT = 4
HALO = 64
TOK_DEV = 128
SAMPLES = 2
POSITIONS = 2048
EXPERTS = 4
CAP = 36
N_EP = 16


def paired_rows(key):
    base = jax.random.fold_in(key, 31)
    key_query, key_keys = jax.random.split(base, 2)
    shape = (SAMPLES, POSITIONS, D)
    key_rows = jnp.clip(jax.random.normal(key_keys, shape, jnp.float32), -4.0, 4.0)
    query_rows = jnp.clip(jax.random.normal(key_query, shape, jnp.float32), -4.0, 4.0)
    return (query_rows, key_rows)


def draw_queries(key, part):
    query_rows, key_rows = paired_rows(key)
    return query_rows.astype(jnp.bfloat16)


def draw_keys(key, part):
    query_rows, key_rows = paired_rows(key)
    return key_rows.astype(jnp.bfloat16)


def set_ends(entries, rng, least, largest):
    shape = entries.shape
    spot = [jax.random.randint(jax.random.fold_in(rng, axis), (), 0, shape[axis]) for axis in range(len(shape))]
    entries = entries.at[tuple(spot)].set(least)
    longest = shape.index(max(shape))
    spot[longest] = (spot[longest] + 1) % shape[longest]
    return entries.at[tuple(spot)].set(largest)


def steps_of(own_key, dims, cuts, least, top_value):
    gain, own = 1.0, jax.random.fold_in(own_key, 6)
    for axis_at, parts in cuts:
        draws = jnp.exp(jax.random.uniform(jax.random.fold_in(own, axis_at), (parts,), jnp.float32, least / len(cuts), top_value / len(cuts)))
        gain = gain * jnp.repeat(draws, dims[axis_at] // parts).reshape([-1 if axis == axis_at else 1 for axis in range(len(dims))])
    return gain


def deal_out(own_key, own, number, rows, number_of, top, reach, skew):
    ranking = jax.random.permutation(own_key, number_of)
    heavy_load, usual = load_shares(number_of, rows * top, reach, skew, True), load_shares(number_of, rows * top, reach, skew, False)
    places = jnp.arange(number_of)

    def named(sizes, rotation):
        used = int((sizes > 0).sum())
        fixed = max(1, used // 4)
        passed = fixed + (places - fixed + rotation * (used - fixed)) % max(1, number_of - fixed)
        return jnp.zeros((number_of,), jnp.int32).at[ranking[jnp.where(places < fixed, places, passed)]].set(jnp.asarray(sizes, jnp.int32))

    sizes = jnp.where(number % 4 == 0, named(heavy_load, number // 4), named(usual, number - number // 4 - 1))
    mixed = jax.random.permutation(jax.random.fold_in(own, 3), number_of)
    source_of, taker = mixed[0:number_of // 2 * 2:2], mixed[1:number_of // 2 * 2:2]
    slack = jnp.minimum(sizes[source_of] - 1, reach - sizes[taker]) // 2
    slack = jnp.where((source_of == ranking[0]) | (taker == ranking[0]) | (sizes[taker] == 0), 0, jnp.maximum(slack, 0))
    passed = jax.random.randint(jax.random.fold_in(own, 4), (number_of // 2,), 0, 1 << 20) % (slack + 1)
    sizes = sizes.at[source_of].add(-passed).at[taker].add(passed)
    members = jnp.searchsorted(jnp.cumsum(sizes), jnp.arange(rows * top), side="right").astype(jnp.int32)
    grid = members.reshape(top, rows).T
    grid = grid[jax.random.permutation(jax.random.fold_in(own, 1), rows)]
    rotation = jax.random.randint(jax.random.fold_in(own, 2), (rows, 1), 0, top)
    return jnp.take_along_axis(grid, (jnp.arange(top)[None, :] + rotation) % top, axis=1)


def load_shares(amount, total, most, slope, full):
    portions = [(1 << 20) // math.isqrt(standing ** slope) + 1 for standing in range(1, amount + 1)]
    largest = most if full else min(most, max(-(-total // amount), total * portions[0] // sum(portions)))
    least = 1 if total - largest >= amount - 1 else 0
    given, spare = [largest] + [least] * (amount - 1), total - largest - least * (amount - 1)
    while spare > 0:
        movable = [i for i in range(1, amount) if given[i] < largest] or [i for i in range(1, amount) if given[i] < most]
        pool, left = sum([portions[i] for i in movable]), spare
        for i in movable:
            more = min(most - given[i], max(1, left * portions[i] // pool), spare)
            given[i] = given[i] + more
            spare = spare - more
    return np.array(given)


def centred(key, shape, deviation, bound, pieces=(), kind=jnp.bfloat16):
    drawn = jax.random.normal(key, shape, jnp.float32) * deviation
    if len(pieces) > 0:
        drawn = steps_of(key, shape, pieces, -0.22, 0.18) * drawn
    return jnp.clip(drawn, min=-bound, max=bound).astype(kind)


def setup_inputs(seed: int = 0) -> dict:
    key_of = jax.random.split(jax.random.key(seed), 10)
    tokens = centred(key_of[0], (SAMPLES, POSITIONS, D), 1.0, 6.0, ((0, 2), (1, 16)))
    queries = draw_queries(jax.random.fold_in(key_of[9], 71), 0)
    keys = draw_keys(jax.random.fold_in(key_of[9], 71), 0)
    values = centred(key_of[3], (SAMPLES, POSITIONS, D), 1.0, 6.0, ((0, 2), (1, 16)))
    key_mask = set_ends((jax.random.randint(key_of[4], (SAMPLES, POSITIONS), 0, 4) < 3).astype(jnp.int32), jax.random.fold_in(key_of[4], 1), 0, 1)
    labels_keys = jax.random.split(jax.random.fold_in(key_of[5], 1), SAMPLES * POSITIONS // TOK_DEV)
    labels_turns = jax.random.permutation(jax.random.fold_in(key_of[5], 3), SAMPLES * POSITIONS // TOK_DEV)
    labels = jax.vmap(lambda own, number: deal_out(jax.random.fold_in(key_of[5], 2), own, number, TOK_DEV, EXPERTS, 1, CAP, 2))(labels_keys, labels_turns).reshape((SAMPLES, POSITIONS, 1))
    cotangent = centred(key_of[6], (SAMPLES, POSITIONS, D), 0.02, 0.125, ((0, 2), (1, 16)))
    weight_in = centred(key_of[7], (D, EXPERTS * FF), D ** -0.5, 0.1875, ((1, 16),))
    weight_out = centred(key_of[8], (EXPERTS * SPLIT, FF // SPLIT, D), FF ** -0.5, 0.09375, ((0, 16),))
    return {"tokens": tokens, "queries": queries, "keys": keys, "values": values, "key_mask": key_mask, "labels": labels, "cotangent": cotangent, "weight_in": weight_in, "weight_out": weight_out}


NEG_FILL = -1e30


def window_attention(query_rows, key_rows, value_rows, mask_rows):
    query_count = query_rows.shape[0]
    key_count = key_rows.shape[0]
    head_width = query_rows.shape[1] // HEADS
    query_heads = query_rows.reshape(query_count, HEADS, head_width).astype(jnp.float32)
    key_heads = key_rows.reshape(key_count, HEADS, head_width).astype(jnp.float32)
    value_heads = value_rows.reshape(key_count, HEADS, head_width).astype(jnp.float32)
    scores = jnp.einsum("qhd,khd->hqk", query_heads, key_heads) * (head_width ** -0.5)
    offset = jnp.arange(key_count, dtype=jnp.int32)[None, :] - HALO - jnp.arange(query_count, dtype=jnp.int32)[:, None]
    usable = (jnp.abs(offset) <= HALO) & ((mask_rows[None, :] == 1) | (offset == 0))
    scores = jnp.where(usable[None], scores, NEG_FILL)
    row_max = jnp.max(scores, axis=-1, keepdims=True)
    raised = jnp.exp(scores - row_max)
    soft_weights = (raised / jnp.sum(raised, axis=-1, keepdims=True)).astype(jnp.bfloat16)
    attended = jnp.einsum("hqk,khd->qhd", soft_weights.astype(jnp.float32), value_heads)
    return attended.reshape(query_count, HEADS * head_width)


def attend_sample(query_sample, key_sample, value_sample, mask_sample):
    key_pad = jnp.pad(key_sample, ((HALO, HALO), (0, 0)))
    value_pad = jnp.pad(value_sample, ((HALO, HALO), (0, 0)))
    mask_pad = jnp.pad(mask_sample, (HALO, HALO))

    def one_block(block_index):
        first_row = block_index * TOK_DEV
        query_block = lax.dynamic_slice_in_dim(query_sample, first_row, TOK_DEV, 0)
        key_block = lax.dynamic_slice_in_dim(key_pad, first_row, TOK_DEV + 2 * HALO, 0)
        value_block = lax.dynamic_slice_in_dim(value_pad, first_row, TOK_DEV + 2 * HALO, 0)
        mask_block = lax.dynamic_slice_in_dim(mask_pad, first_row, TOK_DEV + 2 * HALO, 0)
        return window_attention(query_block, key_block, value_block, mask_block)

    blocks = lax.map(one_block, jnp.arange(N_EP, dtype=jnp.int32))
    return blocks.reshape(POSITIONS, D)


def route_rows(expert_of):
    onehot = (expert_of[:, None] == jnp.arange(EXPERTS, dtype=jnp.int32)[None, :]).astype(jnp.int32)
    running = jnp.cumsum(onehot.reshape(N_EP, TOK_DEV, EXPERTS), axis=1).reshape(POSITIONS, EXPERTS) - 1
    slot_index = jnp.sum(running * onehot, axis=1)
    source = jnp.arange(POSITIONS, dtype=jnp.int32) // TOK_DEV
    return (source * CAP + slot_index).astype(jnp.int32)


def reference(tokens, queries, keys, values, key_mask, labels, cotangent, weight_in, weight_out):
    split_width = FF // SPLIT
    rows_total = N_EP * CAP

    def one_sample(grad_sum, sample):
        sample_tokens, sample_queries, sample_keys, sample_values, sample_mask, sample_labels, sample_cot = sample
        attended = attend_sample(sample_queries, sample_keys, sample_values, sample_mask)
        mixed = (sample_tokens.astype(jnp.float32) + attended).astype(jnp.bfloat16)
        expert_of = sample_labels[:, 0]
        buffer_row = route_rows(expert_of)
        inbound = jnp.zeros((EXPERTS, rows_total, D), jnp.bfloat16).at[expert_of, buffer_row].set(mixed)
        inbound_grad = jnp.zeros((EXPERTS, rows_total, D), jnp.bfloat16).at[expert_of, buffer_row].set(sample_cot)

        def one_expert(expert):
            cols_in = lax.dynamic_slice_in_dim(weight_in, expert * FF, FF, 1)
            rows_out = lax.dynamic_slice_in_dim(weight_out, expert * SPLIT, SPLIT, 0)
            pre_act = jnp.dot(inbound[expert], cols_in, preferred_element_type=jnp.float32)
            hidden = jax.nn.gelu(pre_act).astype(jnp.bfloat16).reshape(rows_total, SPLIT, split_width)
            partial_value = jnp.einsum("rqf,qfd->qrd", hidden.astype(jnp.float32), rows_out.astype(jnp.float32)).astype(jnp.bfloat16)
            combined = jnp.sum(partial_value.astype(jnp.float32), axis=0)
            term = jnp.einsum("rqf,rd->qfd", hidden.astype(jnp.float32), inbound_grad[expert].astype(jnp.float32))
            return combined, term.astype(jnp.bfloat16)

        combined, terms = lax.map(one_expert, jnp.arange(EXPERTS, dtype=jnp.int32))
        expert_out = combined[expert_of, buffer_row]
        layer_rows = (mixed.astype(jnp.float32) + expert_out).astype(jnp.bfloat16)
        grad_sum = grad_sum + terms.reshape(EXPERTS * SPLIT, split_width, D).astype(jnp.float32)
        return grad_sum, layer_rows

    initial = jnp.zeros((EXPERTS * SPLIT, split_width, D), jnp.float32)
    grad_sum, layer_out = lax.scan(one_sample, initial, (tokens, queries, keys, values, key_mask, labels, cotangent))
    return layer_out, grad_sum.astype(jnp.bfloat16)
```

```python
import functools

import jax
import jax.numpy as jnp
from jax import lax
from jax.experimental import pallas as pl
from jax.experimental.pallas import tpu as pltpu
from jax.sharding import PartitionSpec as P

HEADS = 8
SPLIT = 4
HALO = 64
NEG_FILL = -1e30
PARTS = 4
BF16 = jnp.bfloat16
F32 = jnp.float32
VMEM_LIMIT = 48 * 1024 * 1024


def call(body, outs, args, flops=0, **kwargs):
    size = sum(a.size * a.dtype.itemsize for a in args) + sum(o.size * o.dtype.itemsize for o in outs)
    return pl.pallas_call(
        body,
        out_shape=outs,
        compiler_params=pltpu.CompilerParams(vmem_limit_bytes=VMEM_LIMIT),
        cost_estimate=pl.CostEstimate(flops=flops, bytes_accessed=size, transcendentals=0),
        **kwargs,
    )(*args)


def dot(a, b, contract=(1, 0)):
    return lax.dot_general(
        a, b, (((contract[0],), (contract[1],)), ((), ())), preferred_element_type=F32
    )


def out(*shape):
    return jax.ShapeDtypeStruct(shape, BF16)


def iota(shape, dim):
    return lax.broadcasted_iota(jnp.int32, shape, dim)


def one_hot(condition):
    return jnp.where(condition, 1.0, 0.0).astype(BF16)


def halo_body(key_ref, value_ref, mask_ref, up_ref, down_ref):
    rows = key_ref.shape[1]
    width = key_ref.shape[2] // HEADS
    for message, first in ((up_ref, rows - HALO), (down_ref, 0)):
        for head in range(HEADS):
            columns = slice(head * width, (head + 1) * width)
            message[head * HALO : (head + 1) * HALO, :] = key_ref[0, first : first + HALO, columns]
            start = (HEADS + head) * HALO
            message[start : start + HALO, :] = value_ref[0, first : first + HALO, columns]
        mask = mask_ref[:, first : first + HALO].astype(F32)
        mask = jnp.concatenate([mask, jnp.zeros((1, width - HALO), F32)], axis=1)
        message[2 * HEADS * HALO :, :] = jnp.broadcast_to(mask, (16, width)).astype(BF16)


def slots_by_row(labels):
    count = labels.shape[1]
    before = iota((count, count), 0) < iota((count, count), 1)
    as_column = jnp.sum(
        jnp.where(iota((count, count), 0) == iota((count, count), 1), labels, 0), axis=1, keepdims=True
    )
    return jnp.sum(jnp.where(before & (as_column == labels), 1, 0), axis=0, keepdims=True)


def pack(rows, labels, home, message_refs, capacity):
    count, features = rows.shape
    width = features // PARTS
    slot = slots_by_row(labels)
    stacked = jnp.concatenate([rows[:, j * width : (j + 1) * width] for j in range(PARTS)], axis=0)
    height = message_refs[0].shape[0]
    for k, message in enumerate(message_refs):
        mine = labels == (home ^ k)
        places = [
            one_hot(mine & (slot + j * capacity == iota((height, count), 0))) for j in range(PARTS)
        ]
        message[...] = dot(jnp.concatenate(places, axis=1), stacked).astype(BF16)


def pack_body(capacity, rows_ref, label_ref, *message_refs):
    home = lax.axis_index("ep") // SPLIT
    pack(rows_ref[0], label_ref[...], home, message_refs, capacity)


def moving(height, block, count, capacity, which):
    row = iota((height, count * block), 0)
    group = jnp.zeros_like(row)
    for a in range(1, count):
        group += jnp.where(row >= a * capacity, 1, 0)
    inside = row < count * capacity
    return one_hot(inside & (iota(row.shape, 1) == row + group * (block - capacity) + which * capacity))


def assemble_body(capacity, experts, *refs):
    *message_refs, rows_ref = refs
    stacked = jnp.concatenate([m[...] for m in message_refs], axis=0)
    block, width = message_refs[0].shape
    for j in range(PARTS):
        place = moving(rows_ref.shape[0], block, experts, capacity, j)
        rows_ref[:, j * width : (j + 1) * width] = dot(place, stacked).astype(BF16)


def attention_body(
    capacity,
    token_ref,
    query_ref,
    key_ref,
    value_ref,
    mask_ref,
    label_ref,
    before_ref,
    after_ref,
    mixed_ref,
    *message_refs,
):
    rows, features = query_ref.shape[1:]
    width = features // HEADS
    position = lax.axis_index("ep")
    last = lax.axis_size("ep") - 1
    mask_row = 2 * HEADS * HALO
    mask = jnp.concatenate(
        [
            before_ref[mask_row : mask_row + 1, :HALO].astype(F32) * jnp.where(position > 0, 1.0, 0.0),
            mask_ref[...].astype(F32),
            after_ref[mask_row : mask_row + 1, :HALO].astype(F32) * jnp.where(position < last, 1.0, 0.0),
        ],
        axis=1,
    )
    count = rows + 2 * HALO
    offset = iota((rows, count), 1) - HALO - iota((rows, count), 0)
    usable = (jnp.abs(offset) <= HALO) & ((mask > 0.5) | (offset == 0))
    scale = width ** (-0.5)
    for head in range(HEADS):
        columns = slice(head * width, (head + 1) * width)
        at, value_at = head * HALO, (HEADS + head) * HALO
        keys = jnp.concatenate(
            [before_ref[at : at + HALO, :], key_ref[0, :, columns], after_ref[at : at + HALO, :]], axis=0
        )
        values = jnp.concatenate(
            [
                before_ref[value_at : value_at + HALO, :],
                value_ref[0, :, columns],
                after_ref[value_at : value_at + HALO, :],
            ],
            axis=0,
        )
        scores = dot(query_ref[0, :, columns], keys, (1, 1)) * scale
        scores = jnp.where(usable, scores, NEG_FILL)
        raised = jnp.exp(scores - jnp.max(scores, axis=1, keepdims=True))
        soft = (raised * (1.0 / jnp.sum(raised, axis=1, keepdims=True))).astype(BF16)
        mixed_ref[:, columns] = (token_ref[0, :, columns].astype(F32) + dot(soft, values)).astype(BF16)
    home = position // SPLIT
    pack(mixed_ref[...], label_ref[...], home, message_refs, capacity)


def expert_body(*refs):
    row_refs, (in_ref, out_ref), hidden_ref, partial_refs = refs[:SPLIT], refs[SPLIT : SPLIT + 2], refs[SPLIT + 2], refs[SPLIT + 3 :]
    rows = jnp.concatenate([r[...] for r in row_refs], axis=0)
    step = 256
    for at in range(0, in_ref.shape[1], step):
        pre_act = dot(rows, in_ref[:, at : at + step])
        hidden_ref[:, at : at + step] = jax.nn.gelu(pre_act).astype(BF16)
    hidden = hidden_ref[...]
    each = row_refs[0].shape[0]
    for at in range(0, out_ref.shape[2], step):
        partial = dot(hidden, out_ref[0, :, at : at + step]).astype(BF16)
        for k, partial_ref in enumerate(partial_refs):
            partial_ref[:, at : at + step] = partial[k * each : (k + 1) * each]


def combine_body(capacity, experts, *refs):
    partial_refs, message_refs = refs[:SPLIT], refs[SPLIT:]
    total = partial_refs[0][...].astype(F32)
    for p in partial_refs[1:]:
        total += p[...].astype(F32)
    total = total.astype(BF16)
    height, features = total.shape
    width = features // PARTS
    stacked = jnp.concatenate([total[:, j * width : (j + 1) * width] for j in range(PARTS)], axis=0)
    for k, message in enumerate(message_refs):
        place = moving(message.shape[0], height, PARTS, capacity, k)
        message[...] = dot(place, stacked).astype(BF16)


def finish_body(capacity, mixed_ref, label_ref, *refs):
    *message_refs, layer_ref = refs
    home = lax.axis_index("ep") // SPLIT
    labels = label_ref[...]
    count = labels.shape[1]
    slot = slots_by_row(labels)
    block, width = message_refs[0].shape
    stacked = jnp.concatenate([m[...] for m in message_refs], axis=0)
    for j in range(PARTS):
        places = [
            one_hot((labels == (home ^ k)) & (slot + j * capacity == iota((block, count), 0)))
            for k in range(len(message_refs))
        ]
        taken = dot(jnp.concatenate(places, axis=0), stacked, (0, 0))
        columns = slice(j * width, (j + 1) * width)
        layer_ref[0, :, columns] = (mixed_ref[:, columns].astype(F32) + taken).astype(BF16)


def term_body(hidden_ref, *refs):
    *cot_refs, term_ref = refs
    cot = jnp.concatenate([c[...] for c in cot_refs], axis=0)
    step = 256
    for at in range(0, hidden_ref.shape[1], step):
        term_ref[at : at + step, :] = dot(hidden_ref[:, at : at + step], cot, (0, 0)).astype(BF16)


def permute(value, apart):
    return lax.ppermute(value, "ep", [(i, i ^ apart) for i in range(lax.axis_size("ep"))])


def along_line(messages):
    return [messages[0]] + [permute(m, SPLIT * k) for k, m in enumerate(messages) if k > 0]


def in_plane(rows):
    got = {k: permute(rows[k], k) for k in range(SPLIT - 1, 0, -1)}
    return [rows[0]] + [got[k] for k in range(1, SPLIT)]


def shards(tokens, queries, keys, values, key_mask, labels, cotangent, weight_in, weight_out):
    rows_here, features = tokens.shape[1:]
    axis_count = lax.axis_size("ep")
    groups = lax.axis_size("grp")
    experts = axis_count // SPLIT
    capacity = rows_here // experts + max(1, rows_here // (8 * experts))
    width = features // PARTS
    height = -(-PARTS * capacity // 16) * 16
    plane_rows = -(-experts * capacity // 16) * 16
    hidden_units = weight_in.shape[1]
    head_width = features // HEADS
    label_row = labels.reshape(1, rows_here)
    message = out(height, width)

    halo = out(2 * HEADS * HALO + 16, head_width)
    up, down = call(halo_body, (halo, halo), (keys, values, key_mask))
    steps = [(i, i + 1) for i in range(axis_count - 1)]
    before = lax.ppermute(up, "ep", steps)
    after = lax.ppermute(down, "ep", [(j, i) for i, j in steps])

    sent = call(functools.partial(pack_body, capacity), [message] * experts, (cotangent, label_row))
    assemble = functools.partial(assemble_body, capacity, experts)
    (cot_rows,) = call(assemble, [out(plane_rows, features)], along_line(sent))
    cot_all = in_plane([cot_rows] * SPLIT)

    mixed, *sent = call(
        functools.partial(attention_body, capacity),
        [out(rows_here, features)] + [message] * experts,
        (tokens, queries, keys, values, key_mask, label_row, before, after),
        flops=4 * rows_here * (rows_here + 2 * HALO) * features,
    )
    (rows,) = call(assemble, [out(plane_rows, features)], along_line(sent))
    rows_all = in_plane([rows] * SPLIT)

    hidden, *partials = call(
        expert_body,
        [out(SPLIT * plane_rows, hidden_units)] + [out(plane_rows, features)] * SPLIT,
        (*rows_all, weight_in, weight_out),
        flops=4 * SPLIT * plane_rows * features * hidden_units,
    )
    partials = in_plane(partials)
    sent = call(functools.partial(combine_body, capacity, experts), [message] * experts, partials)
    back = along_line(sent)
    (layer_out,) = call(
        functools.partial(finish_body, capacity), [out(1, rows_here, features)], (mixed, label_row, *back)
    )

    (term,) = call(
        term_body,
        [out(hidden_units, features)],
        (hidden, *cot_all),
        flops=2 * SPLIT * plane_rows * features * hidden_units,
    )
    if groups == 2:
        group = lax.axis_index("grp")
        half = hidden_units // 2
        mine = lax.dynamic_slice_in_dim(term, group * half, half, axis=0)
        other = lax.dynamic_slice_in_dim(term, (1 - group) * half, half, axis=0)
        theirs = lax.ppermute(other, "grp", [(0, 1), (1, 0)])
        grad = (mine.astype(F32) + theirs.astype(F32)).astype(BF16)
    else:
        grad = lax.psum_scatter(term, "grp", scatter_dimension=0, tiled=True)
    return (layer_out, grad[None])


def solution(mesh):
    in_specs = (
        P("grp", "ep", None),
        P("grp", "ep", None),
        P("grp", "ep", None),
        P("grp", "ep", None),
        P("grp", "ep"),
        P("grp", "ep", None),
        P("grp", "ep", None),
        P(None, "ep"),
        P("ep", None, None),
    )
    out_specs = (P("grp", "ep", None), P("ep", "grp", None))
    return jax.shard_map(shards, mesh=mesh, in_specs=in_specs, out_specs=out_specs, check_vma=False)
```

```python
import functools

import jax
import jax.numpy as jnp
from jax import lax
from jax.experimental import pallas as pl
from jax.experimental.pallas import tpu as pltpu
from jax.sharding import PartitionSpec as P

HEADS = 8
SPLIT = 4
HALO = 64
NEG_FILL = -1e30
PARTS = 4
STEP = 256
BF16 = jnp.bfloat16
F32 = jnp.float32
VMEM_LIMIT = 48 * 1024 * 1024
HBM = pl.BlockSpec(memory_space=pltpu.HBM)
VMEM = pl.BlockSpec(memory_space=pltpu.VMEM)
ANY = pl.BlockSpec(memory_space=pl.ANY)


def call(body, outs, vmem=(), hbm=(), after=(), scratch=(), flops=0, size=None):
    args = (*vmem, *(pltpu.with_memory_space_constraint(a, pltpu.HBM) for a in hbm), *after)
    n_in, n_after = len(vmem) + len(hbm), len(after)

    def kernel(*refs):
        body(*refs[:n_in], *refs[n_in + n_after :])

    if size is None:
        size = sum(a.size * a.dtype.itemsize for a in (*vmem, *hbm, *outs))
    return pl.pallas_call(
        kernel,
        out_shape=outs,
        in_specs=[VMEM] * len(vmem) + [HBM] * len(hbm) + [ANY] * n_after,
        out_specs=[VMEM] * len(outs),
        scratch_shapes=scratch,
        compiler_params=pltpu.CompilerParams(vmem_limit_bytes=VMEM_LIMIT),
        cost_estimate=pl.CostEstimate(flops=flops, bytes_accessed=size, transcendentals=0),
    )(*args)


def load(pairs, sems):
    copies = [pltpu.make_async_copy(src, dst, sems.at[i]) for i, (src, dst) in enumerate(pairs)]
    for c in copies:
        c.start()
    return copies


def dot(a, b, contract=(1, 0)):
    return lax.dot_general(
        a, b, (((contract[0],), (contract[1],)), ((), ())), preferred_element_type=F32
    )


def out(*shape, dtype=BF16):
    return jax.ShapeDtypeStruct(shape, dtype)


def iota(shape, dim):
    return lax.broadcasted_iota(jnp.int32, shape, dim)


def one_hot(condition):
    return jnp.where(condition, 1.0, 0.0).astype(BF16)


def column_blocks(rows):
    width = rows.shape[1] // PARTS
    return jnp.concatenate([rows[:, j * width : (j + 1) * width] for j in range(PARTS)], axis=0)


def home_plane():
    return lax.axis_index("ep") // SPLIT


def halo_body(key_hbm, value_hbm, mask_hbm, up_ref, down_ref, key_ref, value_ref, mask_ref, sems):
    copies = load(((key_hbm, key_ref), (value_hbm, value_ref), (mask_hbm, mask_ref)), sems)
    for c in copies:
        c.wait()
    rows = key_ref.shape[1]
    width = key_ref.shape[2] // HEADS
    for message, first in ((up_ref, rows - HALO), (down_ref, 0)):
        for head in range(HEADS):
            columns = slice(head * width, (head + 1) * width)
            message[head * HALO : (head + 1) * HALO, :] = key_ref[0, first : first + HALO, columns]
            start = (HEADS + head) * HALO
            message[start : start + HALO, :] = value_ref[0, first : first + HALO, columns]
        mask = mask_ref[:, first : first + HALO].astype(F32)
        mask = jnp.concatenate([mask, jnp.zeros((1, width - HALO), F32)], axis=1)
        message[2 * HEADS * HALO :, :] = jnp.broadcast_to(mask, (16, width)).astype(BF16)


def slots_of(labels):
    count = labels.shape[1]
    row, column = iota((count, count), 0), iota((count, count), 1)
    as_column = jnp.sum(jnp.where(row == column, labels, 0), axis=1, keepdims=True)
    return jnp.sum(jnp.where((row < column) & (as_column == labels), 1, 0), axis=0, keepdims=True)


def pack(rows, labels, slot, message_refs, capacity):
    home = home_plane()
    count = rows.shape[0]
    stacked = column_blocks(rows)
    height = message_refs[0].shape[0]
    for k, message in enumerate(message_refs):
        mine = labels == (home ^ k)
        places = [one_hot(mine & (slot + j * capacity == iota((height, count), 0))) for j in range(PARTS)]
        message[...] = dot(jnp.concatenate(places, axis=1), stacked).astype(BF16)


def pack_body(capacity, cot_hbm, label_hbm, query_hbm, token_hbm, route_ref, query_ref, token_ref, *refs):
    *message_refs, cot_ref, label_ref, sems = refs
    copies = load(
        ((label_hbm, label_ref), (cot_hbm, cot_ref), (query_hbm, query_ref), (token_hbm, token_ref)), sems
    )
    copies[0].wait()
    labels = label_ref[...]
    slot = slots_of(labels)
    route_ref[0:1, :] = labels
    route_ref[1:2, :] = slot
    copies[1].wait()
    pack(cot_ref[0], labels, slot, message_refs, capacity)
    for c in copies[2:]:
        c.wait()


def group_of(row, capacity, experts):
    group = jnp.zeros_like(row)
    for a in range(1, experts):
        group += jnp.where(row >= a * capacity, 1, 0)
    return group


def gather_body(capacity, experts, first_row, first_group, *refs):
    *message_refs, rows_ref = refs
    stacked = jnp.concatenate([m[...] for m in message_refs], axis=0)
    block, width = message_refs[0].shape
    row = iota((rows_ref.shape[0], stacked.shape[0]), 0) + first_row
    group = group_of(row, capacity, experts)
    source = (group - first_group) * block + row - group * capacity
    source = jnp.where(row < experts * capacity, source, -(1 << 20)) - iota(row.shape, 1)
    for j in range(PARTS):
        place = one_hot(source == -j * capacity)
        rows_ref[:, j * width : (j + 1) * width] = dot(place, stacked).astype(BF16)


def scatter(total, groups, message_refs, capacity):
    stacked = column_blocks(total)
    block = total.shape[0]
    height = message_refs[0].shape[0]
    row = iota((height, stacked.shape[0]), 0)
    part = group_of(row, capacity, PARTS)
    source = part * block + row - part * capacity
    source = jnp.where(row < PARTS * capacity, source, -(1 << 20)) - iota(row.shape, 1)
    for group, message in zip(groups, message_refs, strict=True):
        message[...] = dot(one_hot(source == -group * capacity), stacked).astype(BF16)


def added(refs):
    total = refs[0][...].astype(F32)
    for r in refs[1:]:
        total += r[...].astype(F32)
    return total.astype(BF16)


def combine_body(capacity, experts, *refs):
    scatter(added(refs[:SPLIT]), range(experts), refs[SPLIT:], capacity)


def attention_body(
    capacity, query_ref, token_ref, key_ref, value_ref, mask_ref, route_ref, before_ref, after_ref, mixed_ref, *message_refs
):
    rows, features = query_ref.shape[1:]
    width = features // HEADS
    position = lax.axis_index("ep")
    last = lax.axis_size("ep") - 1
    mask_row = 2 * HEADS * HALO
    mask = jnp.concatenate(
        [
            before_ref[mask_row : mask_row + 1, :HALO].astype(F32) * jnp.where(position > 0, 1.0, 0.0),
            mask_ref[...].astype(F32),
            after_ref[mask_row : mask_row + 1, :HALO].astype(F32) * jnp.where(position < last, 1.0, 0.0),
        ],
        axis=1,
    )
    count = rows + 2 * HALO
    offset = iota((rows, count), 1) - HALO - iota((rows, count), 0)
    usable = (jnp.abs(offset) <= HALO) & ((mask > 0.5) | (offset == 0))
    scale = width ** (-0.5)
    for head in range(HEADS):
        columns = slice(head * width, (head + 1) * width)
        at, value_at = head * HALO, (HEADS + head) * HALO
        keys = jnp.concatenate(
            [before_ref[at : at + HALO, :], key_ref[0, :, columns], after_ref[at : at + HALO, :]], axis=0
        )
        values = jnp.concatenate(
            [
                before_ref[value_at : value_at + HALO, :],
                value_ref[0, :, columns],
                after_ref[value_at : value_at + HALO, :],
            ],
            axis=0,
        )
        scores = dot(query_ref[0, :, columns], keys, (1, 1)) * scale
        scores = jnp.where(usable, scores, NEG_FILL)
        raised = jnp.exp(scores - jnp.max(scores, axis=1, keepdims=True))
        soft = (raised * (1.0 / jnp.sum(raised, axis=1, keepdims=True))).astype(BF16)
        mixed_ref[:, columns] = (token_ref[0, :, columns].astype(F32) + dot(soft, values)).astype(BF16)
    pack(mixed_ref[...], route_ref[0:1, :], route_ref[1:2, :], message_refs, capacity)


def expert_body(rows_ref, in_ref, out_ref, hidden_ref, partial_ref):
    rows = rows_ref[...]
    for at in range(0, in_ref.shape[1], STEP):
        hidden_ref[:, at : at + STEP] = jax.nn.gelu(dot(rows, in_ref[:, at : at + STEP])).astype(BF16)
    hidden = hidden_ref[...]
    for at in range(0, out_ref.shape[1], STEP):
        partial_ref[:, at : at + STEP] = dot(hidden, out_ref[:, at : at + STEP]).astype(BF16)


def finish_body(capacity, order, mixed_ref, route_ref, *refs):
    *message_refs, layer_ref = refs
    home = home_plane()
    labels, slot = route_ref[0:1, :], route_ref[1:2, :]
    count = labels.shape[1]
    block, width = message_refs[0].shape
    stacked = jnp.concatenate([m[...] for m in message_refs], axis=0)
    for j in range(PARTS):
        places = [
            one_hot((labels == (home ^ k)) & (slot + j * capacity == iota((block, count), 0))) for k in order
        ]
        taken = dot(jnp.concatenate(places, axis=0), stacked, (0, 0))
        columns = slice(j * width, (j + 1) * width)
        layer_ref[0, :, columns] = (mixed_ref[:, columns].astype(F32) + taken).astype(BF16)


def term_body(side, *refs):
    hidden_refs, cot_refs, rest = refs[:SPLIT], refs[SPLIT : 2 * SPLIT], refs[2 * SPLIT :]
    grad_ref, done_ref = rest[-2:]
    done_ref[...] = jnp.zeros_like(done_ref)
    cot = jnp.concatenate([c[...] for c in cot_refs], axis=0)
    half = hidden_refs[0].shape[1] // 2
    start = (lax.axis_index("grp") ^ side) * half
    for at in range(0, half, STEP):
        columns = pl.ds(pl.multiple_of(start + at, STEP), STEP)
        hidden = jnp.concatenate([h[:, columns] for h in hidden_refs], axis=0)
        term = dot(hidden, cot, (0, 0)).astype(BF16)
        if side == 1:
            grad_ref[at : at + STEP, :] = term
        else:
            theirs = rest[0][at : at + STEP, :].astype(F32)
            grad_ref[0, at : at + STEP, :] = (term.astype(F32) + theirs).astype(BF16)


def whole_term_body(*refs):
    hidden = jnp.concatenate([h[...] for h in refs[:SPLIT]], axis=0)
    cot = jnp.concatenate([c[...] for c in refs[SPLIT : 2 * SPLIT]], axis=0)
    refs[-1][...] = dot(hidden, cot, (0, 0)).astype(BF16)


def permute(value, apart):
    return lax.ppermute(value, "ep", [(i, i ^ apart) for i in range(lax.axis_size("ep"))])


def along_line(messages):
    return [m if k == 0 else permute(m, SPLIT * k) for k, m in enumerate(messages)]


def shards(tokens, queries, keys, values, key_mask, labels, cotangent, weight_in, weight_out):
    rows_here, features = tokens.shape[1:]
    axis_count = lax.axis_size("ep")
    experts = axis_count // SPLIT
    capacity = rows_here // experts + max(1, rows_here // (8 * experts))
    width = features // PARTS
    height = -(-PARTS * capacity // 16) * 16
    plane_rows = -(-experts * capacity // 16) * 16
    hidden_units = weight_in.shape[1]
    head_width = features // HEADS
    label_row = labels.reshape(1, rows_here)
    message = out(height, width)
    block = out(1, rows_here, features)
    row_ints = pltpu.VMEM((1, rows_here), jnp.int32)
    block_scratch = pltpu.VMEM((1, rows_here, features), BF16)

    halo = out(2 * HEADS * HALO + 16, head_width)
    up, down, key_here, value_here, mask_here = call(
        halo_body,
        (halo, halo, block, block, out(1, rows_here, dtype=jnp.int32)),
        hbm=(keys, values, key_mask),
        scratch=[pltpu.SemaphoreType.DMA((3,))],
    )
    steps = [(i, i + 1) for i in range(axis_count - 1)]
    before = lax.ppermute(up, "ep", steps)
    after = lax.ppermute(down, "ep", [(j, i) for i, j in steps])

    gather = functools.partial(gather_body, capacity, experts, 0, 0)
    route, query_here, token_here, *sent = call(
        functools.partial(pack_body, capacity),
        [out(8, rows_here, dtype=jnp.int32), block, block] + [message] * experts,
        hbm=(cotangent, label_row, queries, tokens),
        after=(up,),
        scratch=[block_scratch, row_ints, pltpu.SemaphoreType.DMA((4,))],
        size=0,
    )
    cot_got = along_line(sent)
    in_here, out_here = weight_in, weight_out.reshape(weight_out.shape[1:])

    mixed, *sent = call(
        functools.partial(attention_body, capacity),
        [out(rows_here, features)] + [message] * experts,
        vmem=(query_here, token_here, key_here, value_here, mask_here, route, before, after),
        after=cot_got,
        flops=4 * rows_here * (rows_here + 2 * HALO) * features,
    )

    (cot_rows,) = call(gather, [out(plane_rows, features)], vmem=cot_got, after=(mixed,), size=0)
    cot_x, cot_y = permute(cot_rows, 1), permute(cot_rows, 2)
    (rows,) = call(gather, [out(plane_rows, features)], vmem=along_line(sent))
    cot_xy = permute(cot_x, 2)

    done = [None] * SPLIT
    for k in (0, 3, 1, 2):
        done[k] = call(
            expert_body,
            [out(plane_rows, hidden_units), out(plane_rows, features)],
            vmem=(permute(rows, k) if k else rows, in_here, out_here),
            after=() if k else (cot_x, cot_y),
            flops=4 * plane_rows * features * hidden_units,
        )
    hidden = [d[0] for d in done]

    sums = [permute(d[1], k) if k else d[1] for k, d in enumerate(done)]
    sent = call(functools.partial(combine_body, capacity, experts), [message] * experts, vmem=sums)
    back = along_line(sent)

    inputs = (*hidden, cot_rows, cot_x, cot_y, cot_xy)
    flops = SPLIT * plane_rows * features * hidden_units
    if lax.axis_size("grp") == 2:
        half = hidden_units // 2
        tick = out(8, 128, dtype=F32)
        other, _ = call(
            functools.partial(term_body, 1), [out(half, features), tick], vmem=inputs, after=(sent[0],), flops=flops
        )
        theirs = lax.ppermute(other, "grp", [(0, 1), (1, 0)])
        grad, done = call(
            functools.partial(term_body, 0), [out(1, half, features), tick], vmem=(*inputs, theirs), flops=flops
        )
        ready = (done,)
    else:
        (term,) = call(whole_term_body, [out(hidden_units, features)], vmem=inputs, flops=2 * flops)
        grad = lax.psum_scatter(term, "grp", scatter_dimension=0, tiled=True)[None]
        ready = ()
    (layer_out,) = call(
        functools.partial(finish_body, capacity, range(experts)), [block], vmem=(mixed, route, *back), after=ready
    )
    return (layer_out, grad)


def solution(mesh):
    in_specs = (
        P("grp", "ep", None),
        P("grp", "ep", None),
        P("grp", "ep", None),
        P("grp", "ep", None),
        P("grp", "ep"),
        P("grp", "ep", None),
        P("grp", "ep", None),
        P(None, "ep"),
        P("ep", None, None),
    )
    out_specs = (P("grp", "ep", None), P("ep", "grp", None))
    return jax.shard_map(shards, mesh=mesh, in_specs=in_specs, out_specs=out_specs, check_vma=False)
```

```python
import functools

import jax
import jax.numpy as jnp
from jax import lax
from jax.experimental import pallas as pl
from jax.experimental.pallas import tpu as pltpu
from jax.sharding import PartitionSpec as P

HEADS = 8
SPLIT = 4
HALO = 64
NEG_FILL = -1e30
PARTS = 4
STEP = 256
PIECES = 4
BF16 = jnp.bfloat16
F32 = jnp.float32
VMEM_LIMIT = 48 * 1024 * 1024
HBM = pl.BlockSpec(memory_space=pltpu.HBM)
VMEM = pl.BlockSpec(memory_space=pltpu.VMEM)
ANY = pl.BlockSpec(memory_space=pl.ANY)


def call(body, outs, vmem=(), hbm=(), after=(), scratch=(), flops=0, size=None):
    args = (*vmem, *(pltpu.with_memory_space_constraint(a, pltpu.HBM) for a in hbm), *after)
    n_in, n_after = len(vmem) + len(hbm), len(after)

    def kernel(*refs):
        body(*refs[:n_in], *refs[n_in + n_after :])

    if size is None:
        size = sum(a.size * a.dtype.itemsize for a in (*vmem, *hbm, *outs))
    return pl.pallas_call(
        kernel,
        out_shape=outs,
        in_specs=[VMEM] * len(vmem) + [HBM] * len(hbm) + [ANY] * n_after,
        out_specs=[VMEM] * len(outs),
        scratch_shapes=scratch,
        compiler_params=pltpu.CompilerParams(vmem_limit_bytes=VMEM_LIMIT),
        cost_estimate=pl.CostEstimate(flops=flops, bytes_accessed=size, transcendentals=0),
    )(*args)


def load(pairs, sems):
    copies = [pltpu.make_async_copy(src, dst, sems.at[i]) for i, (src, dst) in enumerate(pairs)]
    for c in copies:
        c.start()
    return copies


def dot(a, b, contract=(1, 0)):
    return lax.dot_general(
        a, b, (((contract[0],), (contract[1],)), ((), ())), preferred_element_type=F32
    )


def out(*shape, dtype=BF16):
    return jax.ShapeDtypeStruct(shape, dtype)


def iota(shape, dim):
    return lax.broadcasted_iota(jnp.int32, shape, dim)


def one_hot(condition):
    return jnp.where(condition, 1.0, 0.0).astype(BF16)


def column_blocks(rows):
    width = rows.shape[1] // PARTS
    return jnp.concatenate([rows[:, j * width : (j + 1) * width] for j in range(PARTS)], axis=0)


def home_plane():
    return lax.axis_index("ep") // SPLIT


def halo_body(key_hbm, value_hbm, mask_hbm, up_ref, down_ref, key_ref, value_ref, mask_ref, sems):
    copies = load(((key_hbm, key_ref), (value_hbm, value_ref), (mask_hbm, mask_ref)), sems)
    for c in copies:
        c.wait()
    rows = key_ref.shape[1]
    width = key_ref.shape[2] // HEADS
    for message, first in ((up_ref, rows - HALO), (down_ref, 0)):
        for head in range(HEADS):
            columns = slice(head * width, (head + 1) * width)
            message[head * HALO : (head + 1) * HALO, :] = key_ref[0, first : first + HALO, columns]
            start = (HEADS + head) * HALO
            message[start : start + HALO, :] = value_ref[0, first : first + HALO, columns]
        mask = mask_ref[:, first : first + HALO].astype(F32)
        mask = jnp.concatenate([mask, jnp.zeros((1, width - HALO), F32)], axis=1)
        message[2 * HEADS * HALO :, :] = jnp.broadcast_to(mask, (16, width)).astype(BF16)


def slots_of(labels):
    count = labels.shape[1]
    row, column = iota((count, count), 0), iota((count, count), 1)
    as_column = jnp.sum(jnp.where(row == column, labels, 0), axis=1, keepdims=True)
    return jnp.sum(jnp.where((row < column) & (as_column == labels), 1, 0), axis=0, keepdims=True)


def pack(rows, labels, slot, message_refs, capacity):
    home = home_plane()
    count = rows.shape[0]
    stacked = column_blocks(rows)
    height = message_refs[0].shape[0]
    for k, message in enumerate(message_refs):
        mine = labels == (home ^ k)
        places = [one_hot(mine & (slot + j * capacity == iota((height, count), 0))) for j in range(PARTS)]
        message[...] = dot(jnp.concatenate(places, axis=1), stacked).astype(BF16)


def pack_body(capacity, cot_hbm, label_hbm, query_hbm, token_hbm, route_ref, query_ref, token_ref, *refs):
    *message_refs, cot_ref, label_ref, sems = refs
    copies = load(
        ((label_hbm, label_ref), (cot_hbm, cot_ref), (query_hbm, query_ref), (token_hbm, token_ref)), sems
    )
    copies[0].wait()
    labels = label_ref[...]
    slot = slots_of(labels)
    route_ref[0:1, :] = labels
    route_ref[1:2, :] = slot
    copies[1].wait()
    pack(cot_ref[0], labels, slot, message_refs, capacity)
    for c in copies[2:]:
        c.wait()


def group_of(row, capacity, experts):
    group = jnp.zeros_like(row)
    for a in range(1, experts):
        group += jnp.where(row >= a * capacity, 1, 0)
    return group


def gather_body(capacity, experts, first_row, first_group, *refs):
    *message_refs, rows_ref = refs
    stacked = jnp.concatenate([m[...] for m in message_refs], axis=0)
    block, width = message_refs[0].shape
    row = iota((rows_ref.shape[0], stacked.shape[0]), 0) + first_row
    group = group_of(row, capacity, experts)
    source = (group - first_group) * block + row - group * capacity
    source = jnp.where(row < experts * capacity, source, -(1 << 20)) - iota(row.shape, 1)
    for j in range(PARTS):
        place = one_hot(source == -j * capacity)
        rows_ref[:, j * width : (j + 1) * width] = dot(place, stacked).astype(BF16)


def scatter(total, groups, message_refs, capacity):
    stacked = column_blocks(total)
    block = total.shape[0]
    height = message_refs[0].shape[0]
    row = iota((height, stacked.shape[0]), 0)
    part = group_of(row, capacity, PARTS)
    source = part * block + row - part * capacity
    source = jnp.where(row < PARTS * capacity, source, -(1 << 20)) - iota(row.shape, 1)
    for group, message in zip(groups, message_refs, strict=True):
        message[...] = dot(one_hot(source == -group * capacity), stacked).astype(BF16)


def add_body(first_ref, second_ref, sum_ref):
    sum_ref[...] = first_ref[...].astype(F32) + second_ref[...].astype(F32)


def combine_body(capacity, experts, sum_ref, last_ref, *message_refs):
    total = (sum_ref[...] + last_ref[...].astype(F32)).astype(BF16)
    scatter(total, range(experts), message_refs, capacity)


def attention_body(
    capacity, query_ref, token_ref, key_ref, value_ref, mask_ref, route_ref, before_ref, after_ref, mixed_ref, *message_refs
):
    rows, features = query_ref.shape[1:]
    width = features // HEADS
    position = lax.axis_index("ep")
    last = lax.axis_size("ep") - 1
    mask_row = 2 * HEADS * HALO
    mask = jnp.concatenate(
        [
            before_ref[mask_row : mask_row + 1, :HALO].astype(F32) * jnp.where(position > 0, 1.0, 0.0),
            mask_ref[...].astype(F32),
            after_ref[mask_row : mask_row + 1, :HALO].astype(F32) * jnp.where(position < last, 1.0, 0.0),
        ],
        axis=1,
    )
    count = rows + 2 * HALO
    offset = iota((rows, count), 1) - HALO - iota((rows, count), 0)
    usable = (jnp.abs(offset) <= HALO) & ((mask > 0.5) | (offset == 0))
    scale = width ** (-0.5)
    for head in range(HEADS):
        columns = slice(head * width, (head + 1) * width)
        at, value_at = head * HALO, (HEADS + head) * HALO
        keys = jnp.concatenate(
            [before_ref[at : at + HALO, :], key_ref[0, :, columns], after_ref[at : at + HALO, :]], axis=0
        )
        values = jnp.concatenate(
            [
                before_ref[value_at : value_at + HALO, :],
                value_ref[0, :, columns],
                after_ref[value_at : value_at + HALO, :],
            ],
            axis=0,
        )
        scores = dot(query_ref[0, :, columns], keys, (1, 1)) * scale
        scores = jnp.where(usable, scores, NEG_FILL)
        raised = jnp.exp(scores - jnp.max(scores, axis=1, keepdims=True))
        soft = (raised * (1.0 / jnp.sum(raised, axis=1, keepdims=True))).astype(BF16)
        mixed_ref[:, columns] = (token_ref[0, :, columns].astype(F32) + dot(soft, values)).astype(BF16)
    pack(mixed_ref[...], route_ref[0:1, :], route_ref[1:2, :], message_refs, capacity)


def expert_body(rows_ref, in_ref, out_ref, hidden_ref, partial_ref):
    rows = rows_ref[...]
    for at in range(0, in_ref.shape[1], STEP):
        hidden_ref[:, at : at + STEP] = jax.nn.gelu(dot(rows, in_ref[:, at : at + STEP])).astype(BF16)
    hidden = hidden_ref[...]
    for at in range(0, out_ref.shape[1], STEP):
        partial_ref[:, at : at + STEP] = dot(hidden, out_ref[:, at : at + STEP]).astype(BF16)


def finish_body(capacity, order, mixed_ref, route_ref, *refs):
    *message_refs, layer_ref = refs
    home = home_plane()
    labels, slot = route_ref[0:1, :], route_ref[1:2, :]
    count = labels.shape[1]
    block, width = message_refs[0].shape
    stacked = jnp.concatenate([m[...] for m in message_refs], axis=0)
    for j in range(PARTS):
        places = [
            one_hot((labels == (home ^ k)) & (slot + j * capacity == iota((block, count), 0))) for k in order
        ]
        taken = dot(jnp.concatenate(places, axis=0), stacked, (0, 0))
        columns = slice(j * width, (j + 1) * width)
        layer_ref[0, :, columns] = (mixed_ref[:, columns].astype(F32) + taken).astype(BF16)


def half_terms(refs, side):
    hidden_refs, cot_refs = refs[:SPLIT], refs[SPLIT : 2 * SPLIT]
    cot = jnp.concatenate([c[...] for c in cot_refs], axis=0)
    half = hidden_refs[0].shape[1] // 2
    start = (lax.axis_index("grp") ^ side) * half
    for at in range(0, half, STEP):
        columns = pl.ds(pl.multiple_of(start + at, STEP), STEP)
        hidden = jnp.concatenate([h[:, columns] for h in hidden_refs], axis=0)
        yield at, dot(hidden, cot, (0, 0)).astype(BF16)


def other_half_body(*refs):
    piece_refs = refs[2 * SPLIT :]
    rows = piece_refs[0].shape[0]
    for at, term in half_terms(refs, 1):
        for r in range(0, STEP, rows):
            piece_refs[(at + r) // rows][...] = term[r : r + rows, :]


def own_half_body(*refs):
    *piece_refs, grad_ref, done_ref = refs[2 * SPLIT :]
    rows = piece_refs[0].shape[0]
    done_ref[...] = jnp.zeros_like(done_ref)
    for at, term in half_terms(refs, 0):
        for r in range(0, STEP, rows):
            theirs = piece_refs[(at + r) // rows][...].astype(F32)
            grad_ref[0, at + r : at + r + rows, :] = (term[r : r + rows, :].astype(F32) + theirs).astype(BF16)


def whole_term_body(*refs):
    hidden = jnp.concatenate([h[...] for h in refs[:SPLIT]], axis=0)
    cot = jnp.concatenate([c[...] for c in refs[SPLIT : 2 * SPLIT]], axis=0)
    refs[-1][...] = dot(hidden, cot, (0, 0)).astype(BF16)


def permute(value, apart):
    return lax.ppermute(value, "ep", [(i, i ^ apart) for i in range(lax.axis_size("ep"))])


def along_line(messages):
    return [m if k == 0 else permute(m, SPLIT * k) for k, m in enumerate(messages)]


def shards(tokens, queries, keys, values, key_mask, labels, cotangent, weight_in, weight_out):
    rows_here, features = tokens.shape[1:]
    axis_count = lax.axis_size("ep")
    experts = axis_count // SPLIT
    capacity = rows_here // experts + max(1, rows_here // (8 * experts))
    width = features // PARTS
    height = -(-PARTS * capacity // 16) * 16
    plane_rows = -(-experts * capacity // 16) * 16
    hidden_units = weight_in.shape[1]
    head_width = features // HEADS
    label_row = labels.reshape(1, rows_here)
    message = out(height, width)
    block = out(1, rows_here, features)
    row_ints = pltpu.VMEM((1, rows_here), jnp.int32)
    block_scratch = pltpu.VMEM((1, rows_here, features), BF16)

    halo = out(2 * HEADS * HALO + 16, head_width)
    up, down, key_here, value_here, mask_here = call(
        halo_body,
        (halo, halo, block, block, out(1, rows_here, dtype=jnp.int32)),
        hbm=(keys, values, key_mask),
        scratch=[pltpu.SemaphoreType.DMA((3,))],
    )
    steps = [(i, i + 1) for i in range(axis_count - 1)]
    before = lax.ppermute(up, "ep", steps)
    after = lax.ppermute(down, "ep", [(j, i) for i, j in steps])

    gather = functools.partial(gather_body, capacity, experts, 0, 0)
    route, query_here, token_here, *sent = call(
        functools.partial(pack_body, capacity),
        [out(8, rows_here, dtype=jnp.int32), block, block] + [message] * experts,
        hbm=(cotangent, label_row, queries, tokens),
        after=(up,),
        scratch=[block_scratch, row_ints, pltpu.SemaphoreType.DMA((4,))],
        size=0,
    )
    cot_got = along_line(sent)
    in_here, out_here = weight_in, weight_out.reshape(weight_out.shape[1:])

    mixed, *sent = call(
        functools.partial(attention_body, capacity),
        [out(rows_here, features)] + [message] * experts,
        vmem=(query_here, token_here, key_here, value_here, mask_here, route, before, after),
        flops=4 * rows_here * (rows_here + 2 * HALO) * features,
    )

    (cot_rows,) = call(gather, [out(plane_rows, features)], vmem=cot_got, after=(mixed,), size=0)
    cot_x, cot_y = permute(cot_rows, 1), permute(cot_rows, 2)
    (rows,) = call(gather, [out(plane_rows, features)], vmem=along_line(sent))
    cot_xy = permute(cot_x, 2)

    own_hidden, own_partial = call(
        expert_body,
        [out(plane_rows, hidden_units), out(plane_rows, features)],
        vmem=(rows, in_here, out_here),
        after=(cot_x, cot_y),
        flops=4 * plane_rows * features * hidden_units,
    )
    hiddens, partials = [own_hidden], []
    for k in (3, 1, 2):
        hidden, partial = call(
            expert_body,
            [out(plane_rows, hidden_units), out(plane_rows, features)],
            vmem=(permute(rows, k), in_here, out_here),
            after=(own_hidden,),
            flops=4 * plane_rows * features * hidden_units,
        )
        hiddens.append(hidden)
        partials.append(partial)

    total = own_partial
    totals = []
    for partial, k in zip(partials[:-1], (3, 1)):
        (total,) = call(
            add_body, [out(plane_rows, features, dtype=F32)], vmem=(total, permute(partial, k)), size=0
        )
        totals.append(total)
    last = permute(partials[-1], 2)
    inputs = (*hiddens, cot_rows, cot_xy, cot_x, cot_y)
    flops = SPLIT * plane_rows * features * hidden_units
    if lax.axis_size("grp") == 2:
        half = hidden_units // 2
        pieces = call(
            other_half_body, [out(half // PIECES, features)] * PIECES, vmem=inputs, after=totals[:1], flops=flops
        )
        theirs = [lax.ppermute(piece, "grp", [(0, 1), (1, 0)]) for piece in pieces]
        grad, done = call(
            own_half_body,
            [out(1, half, features), out(8, 128, dtype=F32)],
            vmem=(*inputs, *theirs),
            flops=flops,
        )
        ready = (done,)
    else:
        (term,) = call(whole_term_body, [out(hidden_units, features)], vmem=inputs, flops=2 * flops)
        grad = lax.psum_scatter(term, "grp", scatter_dimension=0, tiled=True)[None]
        ready = ()
    sent = call(functools.partial(combine_body, capacity, experts), [message] * experts, vmem=(total, last))
    back = along_line(sent)
    (layer_out,) = call(
        functools.partial(finish_body, capacity, range(experts)), [block], vmem=(mixed, route, *back), after=ready
    )
    return (layer_out, grad)


def solution(mesh):
    in_specs = (
        P("grp", "ep", None),
        P("grp", "ep", None),
        P("grp", "ep", None),
        P("grp", "ep", None),
        P("grp", "ep"),
        P("grp", "ep", None),
        P("grp", "ep", None),
        P(None, "ep"),
        P("ep", None, None),
    )
    out_specs = (P("grp", "ep", None), P("ep", "grp", None))
    return jax.shard_map(shards, mesh=mesh, in_specs=in_specs, out_specs=out_specs, check_vma=False)
```

```python
import functools

import jax
import jax.numpy as jnp
from jax import lax
from jax.experimental import pallas as pl
from jax.experimental.pallas import tpu as pltpu
from jax.sharding import PartitionSpec as P

HEADS = 8
SPLIT = 4
HALO = 64
NEG_FILL = -1e30
PARTS = 4
STEP = 256
PIECES = 4
BF16 = jnp.bfloat16
F32 = jnp.float32
VMEM_LIMIT = 48 * 1024 * 1024
HBM = pl.BlockSpec(memory_space=pltpu.HBM)
VMEM = pl.BlockSpec(memory_space=pltpu.VMEM)
ANY = pl.BlockSpec(memory_space=pl.ANY)


def call(body, outs, vmem=(), hbm=(), after=(), scratch=(), flops=0, size=None):
    args = (*vmem, *(pltpu.with_memory_space_constraint(a, pltpu.HBM) for a in hbm), *after)
    n_in, n_after = len(vmem) + len(hbm), len(after)

    def kernel(*refs):
        body(*refs[:n_in], *refs[n_in + n_after :])

    if size is None:
        size = sum(a.size * a.dtype.itemsize for a in (*vmem, *hbm, *outs))
    return pl.pallas_call(
        kernel,
        out_shape=outs,
        in_specs=[VMEM] * len(vmem) + [HBM] * len(hbm) + [ANY] * n_after,
        out_specs=[VMEM] * len(outs),
        scratch_shapes=scratch,
        compiler_params=pltpu.CompilerParams(vmem_limit_bytes=VMEM_LIMIT),
        cost_estimate=pl.CostEstimate(flops=flops, bytes_accessed=size, transcendentals=0),
    )(*args)


def load(pairs, sems):
    copies = [pltpu.make_async_copy(src, dst, sems.at[i]) for i, (src, dst) in enumerate(pairs)]
    for c in copies:
        c.start()
    return copies


def dot(a, b, contract=(1, 0)):
    return lax.dot_general(
        a, b, (((contract[0],), (contract[1],)), ((), ())), preferred_element_type=F32
    )


def out(*shape, dtype=BF16):
    return jax.ShapeDtypeStruct(shape, dtype)


def iota(shape, dim):
    return lax.broadcasted_iota(jnp.int32, shape, dim)


def one_hot(condition):
    return jnp.where(condition, 1.0, 0.0).astype(BF16)


def column_blocks(rows):
    width = rows.shape[1] // PARTS
    return jnp.concatenate([rows[:, j * width : (j + 1) * width] for j in range(PARTS)], axis=0)


def home_plane():
    return lax.axis_index("ep") // SPLIT


def halo_body(key_hbm, value_hbm, mask_hbm, near_out, far_out, key_ref, value_ref, mask_ref, sems):
    copies = load(((key_hbm, key_ref), (value_hbm, value_ref), (mask_hbm, mask_ref)), sems)
    for c in copies:
        c.wait()
    rows = key_ref.shape[1]
    width = key_ref.shape[2] // HEADS
    odd = lax.axis_index("ep") % 2
    for message, last in ((near_out, 1 - odd), (far_out, odd)):
        mine = pl.ds(pl.multiple_of(last * (rows - HALO), HALO), HALO)
        for head in range(HEADS):
            columns = slice(head * width, (head + 1) * width)
            message[head * HALO : (head + 1) * HALO, :] = key_ref[0, mine, columns]
            start = (HEADS + head) * HALO
            message[start : start + HALO, :] = value_ref[0, mine, columns]
        mask = jnp.where(last == 1, mask_ref[:, rows - HALO :], mask_ref[:, :HALO]).astype(F32)
        mask = jnp.concatenate([mask, jnp.zeros((1, width - HALO), F32)], axis=1)
        message[2 * HEADS * HALO :, :] = jnp.broadcast_to(mask, (16, width)).astype(BF16)


def slots_of(labels):
    count = labels.shape[1]
    row, column = iota((count, count), 0), iota((count, count), 1)
    as_column = jnp.sum(jnp.where(row == column, labels, 0), axis=1, keepdims=True)
    return jnp.sum(jnp.where((row < column) & (as_column == labels), 1, 0), axis=0, keepdims=True)


def pack(rows, labels, slot, message_refs, capacity):
    home = home_plane()
    count = rows.shape[0]
    stacked = column_blocks(rows)
    height = message_refs[0].shape[0]
    for p, message in enumerate(message_refs):
        mine = labels == (home ^ (-p % len(message_refs)))
        places = [one_hot(mine & (slot + j * capacity == iota((height, count), 0))) for j in range(PARTS)]
        message[...] = dot(jnp.concatenate(places, axis=1), stacked).astype(BF16)


def pack_body(capacity, cot_hbm, label_hbm, query_hbm, token_hbm, route_ref, query_ref, token_ref, *refs):
    *message_refs, cot_ref, label_ref, sems = refs
    copies = load(
        ((label_hbm, label_ref), (cot_hbm, cot_ref), (query_hbm, query_ref), (token_hbm, token_ref)), sems
    )
    copies[0].wait()
    labels = label_ref[...]
    slot = slots_of(labels)
    route_ref[0:1, :] = labels
    route_ref[1:2, :] = slot
    copies[1].wait()
    pack(cot_ref[0], labels, slot, message_refs, capacity)
    for c in copies[2:]:
        c.wait()


def group_of(row, capacity, experts):
    group = jnp.zeros_like(row)
    for a in range(1, experts):
        group += jnp.where(row >= a * capacity, 1, 0)
    return group


def gather_body(capacity, experts, first_row, first_group, *refs):
    *message_refs, rows_ref = refs
    stacked = jnp.concatenate([m[...] for m in message_refs], axis=0)
    block, width = message_refs[0].shape
    row = iota((rows_ref.shape[0], stacked.shape[0]), 0) + first_row
    group = group_of(row, capacity, experts)
    source = (group - first_group) * block + row - group * capacity
    source = jnp.where(row < experts * capacity, source, -(1 << 20)) - iota(row.shape, 1)
    for j in range(PARTS):
        place = one_hot(source == -j * capacity)
        rows_ref[:, j * width : (j + 1) * width] = dot(place, stacked).astype(BF16)


def scatter(total, groups, message_refs, capacity):
    stacked = column_blocks(total)
    block = total.shape[0]
    height = message_refs[0].shape[0]
    row = iota((height, stacked.shape[0]), 0)
    part = group_of(row, capacity, PARTS)
    source = part * block + row - part * capacity
    source = jnp.where(row < PARTS * capacity, source, -(1 << 20)) - iota(row.shape, 1)
    for group, message in zip(groups, message_refs, strict=True):
        message[...] = dot(one_hot(source == -group * capacity), stacked).astype(BF16)


def add_body(first_ref, second_ref, sum_ref):
    sum_ref[...] = first_ref[...].astype(F32) + second_ref[...].astype(F32)


def combine_body(capacity, experts, sum_ref, last_ref, *message_refs):
    total = (sum_ref[...] + last_ref[...].astype(F32)).astype(BF16)
    scatter(total, range(experts), message_refs, capacity)


def attention_body(
    capacity, query_ref, token_ref, key_ref, value_ref, mask_ref, route_ref, near_ref, far_ref, mixed_ref, *message_refs
):
    rows, features = query_ref.shape[1:]
    width = features // HEADS
    position = lax.axis_index("ep")
    odd = position % 2
    inside = (position > 0) & (position < lax.axis_size("ep") - 1)
    mask_row = 2 * HEADS * HALO
    mask = jnp.concatenate(
        [
            near_ref[mask_row : mask_row + 1, :HALO].astype(F32),
            mask_ref[...].astype(F32),
            far_ref[mask_row : mask_row + 1, :HALO].astype(F32) * jnp.where(inside, 1.0, 0.0),
        ],
        axis=1,
    )
    count = rows + 2 * HALO
    column = iota((rows, count), 1)
    near_first = jnp.where(odd == 1, -HALO, rows)
    far_first = jnp.where(odd == 1, rows, -HALO) - HALO - rows
    first = jnp.where(column < HALO, near_first, jnp.where(column < HALO + rows, -HALO, far_first))
    offset = column + first - iota((rows, count), 0)
    usable = (jnp.abs(offset) <= HALO) & ((mask > 0.5) | (offset == 0))
    scale = width ** (-0.5)
    for head in range(HEADS):
        columns = slice(head * width, (head + 1) * width)
        at, value_at = head * HALO, (HEADS + head) * HALO
        keys = jnp.concatenate(
            [near_ref[at : at + HALO, :], key_ref[0, :, columns], far_ref[at : at + HALO, :]], axis=0
        )
        values = jnp.concatenate(
            [
                near_ref[value_at : value_at + HALO, :],
                value_ref[0, :, columns],
                far_ref[value_at : value_at + HALO, :],
            ],
            axis=0,
        )
        scores = dot(query_ref[0, :, columns], keys, (1, 1)) * scale
        scores = jnp.where(usable, scores, NEG_FILL)
        raised = jnp.exp(scores - jnp.max(scores, axis=1, keepdims=True))
        soft = (raised * (1.0 / jnp.sum(raised, axis=1, keepdims=True))).astype(BF16)
        mixed_ref[:, columns] = (token_ref[0, :, columns].astype(F32) + dot(soft, values)).astype(BF16)
    pack(mixed_ref[...], route_ref[0:1, :], route_ref[1:2, :], message_refs, capacity)


def expert_body(*refs):
    *row_refs, in_ref, out_ref, hidden_ref, partial_ref = refs
    rows = jnp.concatenate([r[...] for r in row_refs], axis=0)
    for at in range(0, in_ref.shape[1], STEP):
        hidden_ref[:, at : at + STEP] = jax.nn.gelu(dot(rows, in_ref[:, at : at + STEP])).astype(BF16)
    hidden = hidden_ref[...]
    for at in range(0, out_ref.shape[1], STEP):
        partial_ref[:, at : at + STEP] = dot(hidden, out_ref[:, at : at + STEP]).astype(BF16)


def finish_body(capacity, mixed_ref, route_ref, *refs):
    *message_refs, layer_ref = refs
    home = home_plane()
    labels, slot = route_ref[0:1, :], route_ref[1:2, :]
    count = labels.shape[1]
    block, width = message_refs[0].shape
    stacked = jnp.concatenate([m[...] for m in message_refs], axis=0)
    for j in range(PARTS):
        places = [
            one_hot((labels == (home ^ (-p % len(message_refs)))) & (slot + j * capacity == iota((block, count), 0)))
            for p in range(len(message_refs))
        ]
        taken = dot(jnp.concatenate(places, axis=0), stacked, (0, 0))
        columns = slice(j * width, (j + 1) * width)
        layer_ref[0, :, columns] = (mixed_ref[:, columns].astype(F32) + taken).astype(BF16)


def half_terms(refs, side):
    hidden_refs, cot_refs = refs[:SPLIT], refs[SPLIT : 2 * SPLIT + 1]
    cot = jnp.concatenate([c[...] for c in cot_refs], axis=0)
    half = hidden_refs[0].shape[1] // 2
    start = (lax.axis_index("grp") ^ side) * half
    for at in range(0, half, STEP):
        columns = pl.ds(pl.multiple_of(start + at, STEP), STEP)
        hidden = jnp.concatenate([h[:, columns] for h in hidden_refs], axis=0)
        yield at, dot(hidden, cot, (0, 0)).astype(BF16)


def other_half_body(*refs):
    piece_refs = refs[2 * SPLIT + 1 :]
    rows = piece_refs[0].shape[0]
    for at, term in half_terms(refs, 1):
        for r in range(0, STEP, rows):
            piece_refs[(at + r) // rows][...] = term[r : r + rows, :]


def own_half_body(*refs):
    *piece_refs, grad_ref, done_ref = refs[2 * SPLIT + 1 :]
    rows = piece_refs[0].shape[0]
    done_ref[...] = jnp.zeros_like(done_ref)
    for at, term in half_terms(refs, 0):
        for r in range(0, STEP, rows):
            theirs = piece_refs[(at + r) // rows][...].astype(F32)
            grad_ref[0, at + r : at + r + rows, :] = (term[r : r + rows, :].astype(F32) + theirs).astype(BF16)


def whole_term_body(*refs):
    hidden = jnp.concatenate([h[...] for h in refs[:SPLIT]], axis=0)
    cot = jnp.concatenate([c[...] for c in refs[SPLIT : 2 * SPLIT + 1]], axis=0)
    refs[-1][...] = dot(hidden, cot, (0, 0)).astype(BF16)


def permute(value, apart):
    return lax.ppermute(value, "ep", [(i, i ^ apart) for i in range(lax.axis_size("ep"))])


def forwarded(along_x, along_y):
    half = along_x.shape[0] // 32 * 16
    return permute(along_x[:half], 2), permute(along_y[half:], 1)


def along_line(messages):
    count = len(messages)
    return [m if p == 0 else permute(m, SPLIT * (count - p)) for p, m in enumerate(messages)]


def shards(tokens, queries, keys, values, key_mask, labels, cotangent, weight_in, weight_out):
    rows_here, features = tokens.shape[1:]
    axis_count = lax.axis_size("ep")
    experts = axis_count // SPLIT
    capacity = rows_here // experts + max(1, rows_here // (8 * experts))
    width = features // PARTS
    height = -(-PARTS * capacity // 16) * 16
    plane_rows = -(-experts * capacity // 16) * 16
    hidden_units = weight_in.shape[1]
    head_width = features // HEADS
    label_row = labels.reshape(1, rows_here)
    message = out(height, width)
    block = out(1, rows_here, features)
    row_ints = pltpu.VMEM((1, rows_here), jnp.int32)
    block_scratch = pltpu.VMEM((1, rows_here, features), BF16)

    halo = out(2 * HEADS * HALO + 16, head_width)
    near, far, key_here, value_here, mask_here = call(
        halo_body,
        (halo, halo, block, block, out(1, rows_here, dtype=jnp.int32)),
        hbm=(keys, values, key_mask),
        scratch=[pltpu.SemaphoreType.DMA((3,))],
    )
    near = permute(near, 1)
    steps = [(i, i + 1) for i in range(1, axis_count - 1, 2)]
    far = lax.ppermute(far, "ep", steps + [(j, i) for i, j in steps])

    gather = functools.partial(gather_body, capacity, experts, 0, 0)
    route, query_here, token_here, *sent = call(
        functools.partial(pack_body, capacity),
        [out(8, rows_here, dtype=jnp.int32), block, block] + [message] * experts,
        hbm=(cotangent, label_row, queries, tokens),
        after=(key_here,),
        scratch=[block_scratch, row_ints, pltpu.SemaphoreType.DMA((4,))],
        size=0,
    )
    cot_got = along_line(sent)
    in_here, out_here = weight_in, weight_out.reshape(weight_out.shape[1:])

    mixed, *sent = call(
        functools.partial(attention_body, capacity),
        [out(rows_here, features)] + [message] * experts,
        vmem=(query_here, token_here, key_here, value_here, mask_here, route, near, far),
        flops=4 * rows_here * (rows_here + 2 * HALO) * features,
    )

    (cot_rows,) = call(gather, [out(plane_rows, features)], vmem=cot_got, after=(mixed,), size=0)
    cot_x, cot_y = permute(cot_rows, 1), permute(cot_rows, 2)
    (rows,) = call(gather, [out(plane_rows, features)], vmem=along_line(sent))
    cot_far = forwarded(cot_x, cot_y)

    row_x, row_y = permute(rows, 1), permute(rows, 2)
    hiddens, partials = [], []
    for pieces, first in (((rows,), (cot_x, cot_y)), ((row_x,), ()), ((row_y,), ()), (forwarded(row_x, row_y), ())):
        hidden, partial = call(
            expert_body,
            [out(plane_rows, hidden_units), out(plane_rows, features)],
            vmem=(*pieces, in_here, out_here),
            after=(*first, *hiddens[:1]),
            flops=4 * plane_rows * features * hidden_units,
        )
        hiddens.append(hidden)
        partials.append(partial)

    total = partials[0]
    totals = []
    for k in (1, 2):
        (total,) = call(
            add_body, [out(plane_rows, features, dtype=F32)], vmem=(total, permute(partials[k], k)), size=0
        )
        totals.append(total)
    last = permute(partials[3], 3)
    inputs = (*hiddens, cot_rows, cot_x, cot_y, *cot_far)
    flops = SPLIT * plane_rows * features * hidden_units
    if lax.axis_size("grp") == 2:
        half = hidden_units // 2
        pieces = call(
            other_half_body, [out(half // PIECES, features)] * PIECES, vmem=inputs, after=totals[:1], flops=flops
        )
        theirs = [lax.ppermute(piece, "grp", [(0, 1), (1, 0)]) for piece in pieces]
        grad, done = call(
            own_half_body,
            [out(1, half, features), out(8, 128, dtype=F32)],
            vmem=(*inputs, *theirs),
            flops=flops,
        )
        ready = (done,)
    else:
        (term,) = call(whole_term_body, [out(hidden_units, features)], vmem=inputs, flops=2 * flops)
        grad = lax.psum_scatter(term, "grp", scatter_dimension=0, tiled=True)[None]
        ready = ()
    sent = call(functools.partial(combine_body, capacity, experts), [message] * experts, vmem=(total, last))
    back = along_line(sent)
    (layer_out,) = call(
        functools.partial(finish_body, capacity), [block], vmem=(mixed, route, *back), after=ready
    )
    return (layer_out, grad)


def solution(mesh):
    in_specs = (
        P("grp", "ep", None),
        P("grp", "ep", None),
        P("grp", "ep", None),
        P("grp", "ep", None),
        P("grp", "ep"),
        P("grp", "ep", None),
        P("grp", "ep", None),
        P(None, "ep"),
        P("ep", None, None),
    )
    out_specs = (P("grp", "ep", None), P("ep", "grp", None))
    return jax.shard_map(shards, mesh=mesh, in_specs=in_specs, out_specs=out_specs, check_vma=False)
```

```python
import functools

import jax
import jax.numpy as jnp
from jax import lax
from jax.experimental import pallas as pl
from jax.experimental.pallas import tpu as pltpu
from jax.sharding import PartitionSpec as P

HEADS = 8
SPLIT = 4
HALO = 64
NEG_FILL = -1e30
PARTS = 4
STEP = 256
PIECES = 4
BF16 = jnp.bfloat16
F32 = jnp.float32
VMEM_LIMIT = 48 * 1024 * 1024
HBM = pl.BlockSpec(memory_space=pltpu.HBM)
VMEM = pl.BlockSpec(memory_space=pltpu.VMEM)
ANY = pl.BlockSpec(memory_space=pl.ANY)


def call(body, outs, vmem=(), hbm=(), after=(), scratch=(), flops=0, size=None):
    args = (*vmem, *(pltpu.with_memory_space_constraint(a, pltpu.HBM) for a in hbm), *after)
    n_in, n_after = len(vmem) + len(hbm), len(after)

    def kernel(*refs):
        body(*refs[:n_in], *refs[n_in + n_after :])

    if size is None:
        size = sum(a.size * a.dtype.itemsize for a in (*vmem, *hbm, *outs))
    return pl.pallas_call(
        kernel,
        out_shape=outs,
        in_specs=[VMEM] * len(vmem) + [HBM] * len(hbm) + [ANY] * n_after,
        out_specs=[VMEM] * len(outs),
        scratch_shapes=scratch,
        compiler_params=pltpu.CompilerParams(vmem_limit_bytes=VMEM_LIMIT),
        cost_estimate=pl.CostEstimate(flops=flops, bytes_accessed=size, transcendentals=0),
    )(*args)


def load(pairs, sems):
    copies = [pltpu.make_async_copy(src, dst, sems.at[i]) for i, (src, dst) in enumerate(pairs)]
    for c in copies:
        c.start()
    return copies


def dot(a, b, contract=(1, 0)):
    return lax.dot_general(
        a, b, (((contract[0],), (contract[1],)), ((), ())), preferred_element_type=F32
    )


def out(*shape, dtype=BF16):
    return jax.ShapeDtypeStruct(shape, dtype)


def iota(shape, dim):
    return lax.broadcasted_iota(jnp.int32, shape, dim)


def one_hot(condition):
    return jnp.where(condition, 1.0, 0.0).astype(BF16)


def column_blocks(rows):
    width = rows.shape[1] // PARTS
    return jnp.concatenate([rows[:, j * width : (j + 1) * width] for j in range(PARTS)], axis=0)


def home_plane():
    return lax.axis_index("ep") // SPLIT


def halo_body(key_hbm, value_hbm, mask_hbm, near_out, far_out, key_ref, value_ref, mask_ref, sems):
    copies = load(((key_hbm, key_ref), (value_hbm, value_ref), (mask_hbm, mask_ref)), sems)
    for c in copies:
        c.wait()
    rows = key_ref.shape[1]
    width = key_ref.shape[2] // HEADS
    odd = lax.axis_index("ep") % 2
    for message, last in ((near_out, 1 - odd), (far_out, odd)):
        mine = pl.ds(pl.multiple_of(last * (rows - HALO), HALO), HALO)
        for head in range(HEADS):
            columns = slice(head * width, (head + 1) * width)
            message[head * HALO : (head + 1) * HALO, :] = key_ref[0, mine, columns]
            start = (HEADS + head) * HALO
            message[start : start + HALO, :] = value_ref[0, mine, columns]
        mask = jnp.where(last == 1, mask_ref[:, rows - HALO :], mask_ref[:, :HALO]).astype(F32)
        mask = jnp.concatenate([mask, jnp.zeros((1, width - HALO), F32)], axis=1)
        message[2 * HEADS * HALO :, :] = jnp.broadcast_to(mask, (16, width)).astype(BF16)


def slots_of(labels):
    count = labels.shape[1]
    row, column = iota((count, count), 0), iota((count, count), 1)
    as_column = jnp.sum(jnp.where(row == column, labels, 0), axis=1, keepdims=True)
    return jnp.sum(jnp.where((row < column) & (as_column == labels), 1, 0), axis=0, keepdims=True)


def pack(rows, labels, slot, message_refs, capacity):
    home = home_plane()
    count = rows.shape[0]
    stacked = column_blocks(rows)
    height = message_refs[0].shape[0]
    for p, message in enumerate(message_refs):
        mine = labels == (home ^ p)
        places = [one_hot(mine & (slot + j * capacity == iota((height, count), 0))) for j in range(PARTS)]
        message[...] = dot(jnp.concatenate(places, axis=1), stacked).astype(BF16)


def pack_body(capacity, cot_hbm, label_hbm, query_hbm, token_hbm, route_ref, query_ref, token_ref, *refs):
    *message_refs, cot_ref, label_ref, sems = refs
    copies = load(
        ((label_hbm, label_ref), (cot_hbm, cot_ref), (query_hbm, query_ref), (token_hbm, token_ref)), sems
    )
    copies[0].wait()
    labels = label_ref[...]
    slot = slots_of(labels)
    route_ref[0:1, :] = labels
    route_ref[1:2, :] = slot
    copies[1].wait()
    pack(cot_ref[0], labels, slot, message_refs, capacity)
    for c in copies[2:]:
        c.wait()


def group_of(row, capacity, experts):
    group = jnp.zeros_like(row)
    for a in range(1, experts):
        group += jnp.where(row >= a * capacity, 1, 0)
    return group


def gather_body(capacity, experts, order, *refs):
    *message_refs, rows_ref = refs
    message_refs = [message_refs[order.index(k)] for k in range(experts)]
    stacked = jnp.concatenate([m[...] for m in message_refs], axis=0)
    block, width = message_refs[0].shape
    row = iota((rows_ref.shape[0], stacked.shape[0]), 0)
    group = group_of(row, capacity, experts)
    source = group * block + row - group * capacity
    source = jnp.where(row < experts * capacity, source, -(1 << 20)) - iota(row.shape, 1)
    for j in range(PARTS):
        place = one_hot(source == -j * capacity)
        rows_ref[:, j * width : (j + 1) * width] = dot(place, stacked).astype(BF16)


def scatter(total, groups, message_refs, capacity):
    stacked = column_blocks(total)
    block = total.shape[0]
    height = message_refs[0].shape[0]
    row = iota((height, stacked.shape[0]), 0)
    part = group_of(row, capacity, PARTS)
    source = part * block + row - part * capacity
    source = jnp.where(row < PARTS * capacity, source, -(1 << 20)) - iota(row.shape, 1)
    for group, message in zip(groups, message_refs, strict=True):
        message[...] = dot(one_hot(source == -group * capacity), stacked).astype(BF16)


def add_body(first_ref, second_ref, sum_ref):
    sum_ref[...] = first_ref[...].astype(F32) + second_ref[...].astype(F32)


def combine_body(capacity, experts, sum_ref, last_ref, *message_refs):
    total = (sum_ref[...] + last_ref[...].astype(F32)).astype(BF16)
    scatter(total, range(experts), message_refs, capacity)


def attention_body(
    capacity, query_ref, token_ref, key_ref, value_ref, mask_ref, route_ref, near_ref, far_ref, mixed_ref, *message_refs
):
    rows, features = query_ref.shape[1:]
    width = features // HEADS
    position = lax.axis_index("ep")
    odd = position % 2
    inside = (position > 0) & (position < lax.axis_size("ep") - 1)
    mask_row = 2 * HEADS * HALO
    mask = jnp.concatenate(
        [
            near_ref[mask_row : mask_row + 1, :HALO].astype(F32),
            mask_ref[...].astype(F32),
            far_ref[mask_row : mask_row + 1, :HALO].astype(F32) * jnp.where(inside, 1.0, 0.0),
        ],
        axis=1,
    )
    count = rows + 2 * HALO
    column = iota((rows, count), 1)
    near_first = jnp.where(odd == 1, -HALO, rows)
    far_first = jnp.where(odd == 1, rows, -HALO) - HALO - rows
    first = jnp.where(column < HALO, near_first, jnp.where(column < HALO + rows, -HALO, far_first))
    offset = column + first - iota((rows, count), 0)
    usable = (jnp.abs(offset) <= HALO) & ((mask > 0.5) | (offset == 0))
    scale = width ** (-0.5)
    for head in range(HEADS):
        columns = slice(head * width, (head + 1) * width)
        at, value_at = head * HALO, (HEADS + head) * HALO
        keys = jnp.concatenate(
            [near_ref[at : at + HALO, :], key_ref[0, :, columns], far_ref[at : at + HALO, :]], axis=0
        )
        values = jnp.concatenate(
            [
                near_ref[value_at : value_at + HALO, :],
                value_ref[0, :, columns],
                far_ref[value_at : value_at + HALO, :],
            ],
            axis=0,
        )
        scores = dot(query_ref[0, :, columns], keys, (1, 1)) * scale
        scores = jnp.where(usable, scores, NEG_FILL)
        raised = jnp.exp(scores - jnp.max(scores, axis=1, keepdims=True))
        soft = (raised * (1.0 / jnp.sum(raised, axis=1, keepdims=True))).astype(BF16)
        mixed_ref[:, columns] = (token_ref[0, :, columns].astype(F32) + dot(soft, values)).astype(BF16)
    pack(mixed_ref[...], route_ref[0:1, :], route_ref[1:2, :], message_refs, capacity)


def expert_body(*refs):
    *row_refs, in_ref, out_ref, hidden_ref, partial_ref = refs
    rows = jnp.concatenate([r[...] for r in row_refs], axis=0)
    for at in range(0, in_ref.shape[1], STEP):
        hidden_ref[:, at : at + STEP] = jax.nn.gelu(dot(rows, in_ref[:, at : at + STEP])).astype(BF16)
    hidden = hidden_ref[...]
    for at in range(0, out_ref.shape[1], STEP):
        partial_ref[:, at : at + STEP] = dot(hidden, out_ref[:, at : at + STEP]).astype(BF16)


def finish_body(capacity, order, mixed_ref, route_ref, *refs):
    *message_refs, layer_ref = refs
    message_refs = [message_refs[order.index(k)] for k in range(len(message_refs))]
    home = home_plane()
    labels, slot = route_ref[0:1, :], route_ref[1:2, :]
    count = labels.shape[1]
    block, width = message_refs[0].shape
    stacked = jnp.concatenate([m[...] for m in message_refs], axis=0)
    for j in range(PARTS):
        places = [
            one_hot((labels == (home ^ p)) & (slot + j * capacity == iota((block, count), 0)))
            for p in range(len(message_refs))
        ]
        taken = dot(jnp.concatenate(places, axis=0), stacked, (0, 0))
        columns = slice(j * width, (j + 1) * width)
        layer_ref[0, :, columns] = (mixed_ref[:, columns].astype(F32) + taken).astype(BF16)


def half_terms(refs, side):
    hidden_refs, cot_refs = refs[:SPLIT], refs[SPLIT : 2 * SPLIT + 1]
    cot = jnp.concatenate([c[...] for c in cot_refs], axis=0)
    half = hidden_refs[0].shape[1] // 2
    start = (lax.axis_index("grp") ^ side) * half
    for at in range(0, half, STEP):
        columns = pl.ds(pl.multiple_of(start + at, STEP), STEP)
        hidden = jnp.concatenate([h[:, columns] for h in hidden_refs], axis=0)
        yield at, dot(hidden, cot, (0, 0)).astype(BF16)


def other_half_body(*refs):
    piece_refs = refs[2 * SPLIT + 1 :]
    rows = piece_refs[0].shape[0]
    for at, term in half_terms(refs, 1):
        for r in range(0, STEP, rows):
            piece_refs[(at + r) // rows][...] = term[r : r + rows, :]


def own_half_body(*refs):
    *piece_refs, grad_ref, done_ref = refs[2 * SPLIT + 1 :]
    rows = piece_refs[0].shape[0]
    done_ref[...] = jnp.zeros_like(done_ref)
    for at, term in half_terms(refs, 0):
        for r in range(0, STEP, rows):
            theirs = piece_refs[(at + r) // rows][...].astype(F32)
            grad_ref[0, at + r : at + r + rows, :] = (term[r : r + rows, :].astype(F32) + theirs).astype(BF16)


def whole_term_body(*refs):
    hidden = jnp.concatenate([h[...] for h in refs[:SPLIT]], axis=0)
    cot = jnp.concatenate([c[...] for c in refs[SPLIT : 2 * SPLIT + 1]], axis=0)
    refs[-1][...] = dot(hidden, cot, (0, 0)).astype(BF16)


def permute(value, apart):
    return lax.ppermute(value, "ep", [(i, i ^ apart) for i in range(lax.axis_size("ep"))])


def forwarded(along_x, along_y):
    half = along_x.shape[0] // 32 * 16
    return permute(along_x[:half], 2), permute(along_y[half:], 1)


def along_line(messages):
    return [m if k == 0 else permute(m, SPLIT * k) for k, m in enumerate(messages)]


def shards(tokens, queries, keys, values, key_mask, labels, cotangent, weight_in, weight_out):
    rows_here, features = tokens.shape[1:]
    axis_count = lax.axis_size("ep")
    experts = axis_count // SPLIT
    capacity = rows_here // experts + max(1, rows_here // (8 * experts))
    width = features // PARTS
    height = -(-PARTS * capacity // 16) * 16
    plane_rows = -(-experts * capacity // 16) * 16
    hidden_units = weight_in.shape[1]
    head_width = features // HEADS
    label_row = labels.reshape(1, rows_here)
    message = out(height, width)
    block = out(1, rows_here, features)
    row_ints = pltpu.VMEM((1, rows_here), jnp.int32)
    block_scratch = pltpu.VMEM((1, rows_here, features), BF16)

    halo = out(2 * HEADS * HALO + 16, head_width)
    near, far, key_here, value_here, mask_here = call(
        halo_body,
        (halo, halo, block, block, out(1, rows_here, dtype=jnp.int32)),
        hbm=(keys, values, key_mask),
        scratch=[pltpu.SemaphoreType.DMA((3,))],
    )
    near = permute(near, 1)
    steps = [(i, i + 1) for i in range(1, axis_count - 1, 2)]
    far = lax.ppermute(far, "ep", steps + [(j, i) for i, j in steps])

    gather = functools.partial(gather_body, capacity, experts)
    route, query_here, token_here, *sent = call(
        functools.partial(pack_body, capacity),
        [out(8, rows_here, dtype=jnp.int32), block, block] + [message] * experts,
        hbm=(cotangent, label_row, queries, tokens),
        after=(key_here,),
        scratch=[block_scratch, row_ints, pltpu.SemaphoreType.DMA((4,))],
        size=0,
    )
    cot_got = along_line(sent)
    in_here, out_here = weight_in, weight_out.reshape(weight_out.shape[1:])

    mixed, *sent = call(
        functools.partial(attention_body, capacity),
        [out(rows_here, features)] + [message] * experts,
        vmem=(query_here, token_here, key_here, value_here, mask_here, route, near, far),
        flops=4 * rows_here * (rows_here + 2 * HALO) * features,
    )

    (cot_rows,) = call(
        functools.partial(gather, range(experts)), [out(plane_rows, features)], vmem=cot_got, after=(mixed,), size=0
    )
    cot_x, cot_y = permute(cot_rows, 1), permute(cot_rows, 2)
    mixed_got = along_line(sent)
    order = [0, *range(2, experts), 1]
    (rows,) = call(
        functools.partial(gather, order), [out(plane_rows, features)], vmem=[mixed_got[k] for k in order]
    )
    cot_far = forwarded(cot_x, cot_y)

    row_x, row_y = permute(rows, 1), permute(rows, 2)
    hiddens, partials = [], []
    for pieces, first in (((rows,), (cot_x, cot_y)), ((row_x,), ()), ((row_y,), ()), (forwarded(row_x, row_y), ())):
        hidden, partial = call(
            expert_body,
            [out(plane_rows, hidden_units), out(plane_rows, features)],
            vmem=(*pieces, in_here, out_here),
            after=(*first, *hiddens[:1]),
            flops=4 * plane_rows * features * hidden_units,
        )
        hiddens.append(hidden)
        partials.append(partial)

    total = partials[0]
    totals = []
    for k in (1, 2):
        (total,) = call(
            add_body, [out(plane_rows, features, dtype=F32)], vmem=(total, permute(partials[k], k)), size=0
        )
        totals.append(total)
    last = permute(partials[3], 3)
    inputs = (*hiddens, cot_rows, cot_x, cot_y, *cot_far)
    flops = SPLIT * plane_rows * features * hidden_units
    if lax.axis_size("grp") == 2:
        half = hidden_units // 2
        pieces = call(
            other_half_body, [out(half // PIECES, features)] * PIECES, vmem=inputs, after=totals[:1], flops=flops
        )
        theirs = [lax.ppermute(piece, "grp", [(0, 1), (1, 0)]) for piece in pieces]
        grad, done = call(
            own_half_body,
            [out(1, half, features), out(8, 128, dtype=F32)],
            vmem=(*inputs, *theirs),
            flops=flops,
        )
        ready = (done,)
    else:
        (term,) = call(whole_term_body, [out(hidden_units, features)], vmem=inputs, flops=2 * flops)
        grad = lax.psum_scatter(term, "grp", scatter_dimension=0, tiled=True)[None]
        ready = ()
    sent = call(functools.partial(combine_body, capacity, experts), [message] * experts, vmem=(total, last))
    back = along_line(sent)
    order = [0, *range(experts - 1, 0, -1)]
    (layer_out,) = call(
        functools.partial(finish_body, capacity, order), [block], vmem=(mixed, route, *[back[k] for k in order]), after=ready
    )
    return (layer_out, grad)


def solution(mesh):
    in_specs = (
        P("grp", "ep", None),
        P("grp", "ep", None),
        P("grp", "ep", None),
        P("grp", "ep", None),
        P("grp", "ep"),
        P("grp", "ep", None),
        P("grp", "ep", None),
        P(None, "ep"),
        P("ep", None, None),
    )
    out_specs = (P("grp", "ep", None), P("ep", "grp", None))
    return jax.shard_map(shards, mesh=mesh, in_specs=in_specs, out_specs=out_specs, check_vma=False)
```

```python
import functools

import jax
import jax.numpy as jnp
from jax import lax
from jax.experimental import pallas as pl
from jax.experimental.pallas import tpu as pltpu
from jax.sharding import PartitionSpec as P

HEADS = 8
SPLIT = 4
HALO = 64
NEG_FILL = -1e30
PARTS = 4
STEP = 256
PIECES = 4
BF16 = jnp.bfloat16
F32 = jnp.float32
VMEM_LIMIT = 48 * 1024 * 1024
HBM = pl.BlockSpec(memory_space=pltpu.HBM)
VMEM = pl.BlockSpec(memory_space=pltpu.VMEM)
ANY = pl.BlockSpec(memory_space=pl.ANY)


def call(body, outs, vmem=(), hbm=(), after=(), scratch=(), flops=0, size=None):
    args = (*vmem, *(pltpu.with_memory_space_constraint(a, pltpu.HBM) for a in hbm), *after)
    n_in, n_after = len(vmem) + len(hbm), len(after)

    def kernel(*refs):
        body(*refs[:n_in], *refs[n_in + n_after :])

    if size is None:
        size = sum(a.size * a.dtype.itemsize for a in (*vmem, *hbm, *outs))
    return pl.pallas_call(
        kernel,
        out_shape=outs,
        in_specs=[VMEM] * len(vmem) + [HBM] * len(hbm) + [ANY] * n_after,
        out_specs=[VMEM] * len(outs),
        scratch_shapes=scratch,
        compiler_params=pltpu.CompilerParams(vmem_limit_bytes=VMEM_LIMIT),
        cost_estimate=pl.CostEstimate(flops=flops, bytes_accessed=size, transcendentals=0),
    )(*args)


def load(pairs, sems):
    copies = [pltpu.make_async_copy(src, dst, sems.at[i]) for i, (src, dst) in enumerate(pairs)]
    for c in copies:
        c.start()
    return copies


def dot(a, b, contract=(1, 0)):
    return lax.dot_general(
        a, b, (((contract[0],), (contract[1],)), ((), ())), preferred_element_type=F32
    )


def out(*shape, dtype=BF16):
    return jax.ShapeDtypeStruct(shape, dtype)


def iota(shape, dim):
    return lax.broadcasted_iota(jnp.int32, shape, dim)


def one_hot(condition):
    return jnp.where(condition, 1.0, 0.0).astype(BF16)


def column_blocks(rows):
    width = rows.shape[1] // PARTS
    return jnp.concatenate([rows[:, j * width : (j + 1) * width] for j in range(PARTS)], axis=0)


def home_plane():
    return lax.axis_index("ep") // SPLIT


def halo_body(key_hbm, value_hbm, mask_hbm, near_out, far_out, key_ref, value_ref, mask_ref, sems):
    copies = load(((key_hbm, key_ref), (value_hbm, value_ref), (mask_hbm, mask_ref)), sems)
    for c in copies:
        c.wait()
    rows = key_ref.shape[1]
    width = key_ref.shape[2] // HEADS
    odd = lax.axis_index("ep") % 2
    for message, last in ((near_out, 1 - odd), (far_out, odd)):
        mine = pl.ds(pl.multiple_of(last * (rows - HALO), HALO), HALO)
        for head in range(HEADS):
            columns = slice(head * width, (head + 1) * width)
            message[head * HALO : (head + 1) * HALO, :] = key_ref[0, mine, columns]
            start = (HEADS + head) * HALO
            message[start : start + HALO, :] = value_ref[0, mine, columns]
        mask = jnp.where(last == 1, mask_ref[:, rows - HALO :], mask_ref[:, :HALO]).astype(F32)
        mask = jnp.concatenate([mask, jnp.zeros((1, width - HALO), F32)], axis=1)
        message[2 * HEADS * HALO :, :] = jnp.broadcast_to(mask, (16, width)).astype(BF16)


def routed(labels):
    count = labels.shape[1]
    row, column = iota((count, count), 0), iota((count, count), 1)
    as_column = jnp.sum(jnp.where(row == column, labels, 0), axis=1, keepdims=True)
    same = as_column == labels
    slot = jnp.sum(jnp.where((row < column) & same, 1, 0), axis=0, keepdims=True)
    return as_column, slot, jnp.sum(jnp.where((column < row) & same, 1, 0), axis=1, keepdims=True)


def to_messages(rows, message_refs, pitch):
    height, width = message_refs[0].shape
    for p, message in enumerate(message_refs):
        for j in range(PARTS):
            start = j * (height // PARTS)
            message[start : start + pitch, :] = rows[p * pitch : (p + 1) * pitch, j * width : (j + 1) * width]


def from_messages(message_refs, pitch, height):
    step, width = message_refs[0].shape[0] // PARTS, message_refs[0].shape[1]
    columns = []
    for j in range(PARTS):
        blocks = [m[j * step : j * step + pitch, :] for m in message_refs]
        spare = height - pitch * len(blocks)
        columns.append(jnp.concatenate(blocks + [jnp.zeros((spare, width), BF16)] * (spare > 0), axis=0))
    return columns


def pack(rows, place_ref, message_refs, pitch):
    to_messages(dot(place_ref[...], rows).astype(BF16), message_refs, pitch)


def pack_body(pitch, cot_hbm, label_hbm, query_hbm, token_hbm, place_ref, back_ref, query_ref, token_ref, *refs):
    *message_refs, cot_ref, label_ref, sems = refs
    copies = load(
        ((label_hbm, label_ref), (cot_hbm, cot_ref), (query_hbm, query_ref), (token_hbm, token_ref)), sems
    )
    copies[0].wait()
    labels = label_ref[...]
    label_column, slot, slot_column = routed(labels)
    home = home_plane()
    place_ref[...] = one_hot((labels ^ home) * pitch + slot == iota(place_ref.shape, 0))
    back_ref[...] = one_hot((label_column ^ home) * pitch + slot_column == iota(back_ref.shape, 1))
    copies[1].wait()
    pack(cot_ref[0], place_ref, message_refs, pitch)
    for c in copies[2:]:
        c.wait()


def gather_body(order, pitch, *refs):
    *message_refs, rows_ref = refs
    width = message_refs[0].shape[1]
    ordered = [message_refs[order.index(k)] for k in range(len(order))]
    for j, column in enumerate(from_messages(ordered, pitch, rows_ref.shape[0])):
        rows_ref[:, j * width : (j + 1) * width] = column


def combine_body(pitch, *refs):
    partial_refs, message_refs = refs[:SPLIT], refs[SPLIT:]
    total = partial_refs[0][...].astype(F32)
    for partial_ref in partial_refs[1:]:
        total += partial_ref[...].astype(F32)
    to_messages(total.astype(BF16), message_refs, pitch)


def attention_body(
    pitch, query_ref, token_ref, key_ref, value_ref, mask_ref, near_ref, far_ref, place_ref, mixed_ref, *message_refs
):
    rows, features = query_ref.shape[1:]
    width = features // HEADS
    position = lax.axis_index("ep")
    odd = position % 2
    inside = (position > 0) & (position < lax.axis_size("ep") - 1)
    mask_row = 2 * HEADS * HALO
    mask = jnp.concatenate(
        [
            near_ref[mask_row : mask_row + 1, :HALO].astype(F32),
            mask_ref[...].astype(F32),
            far_ref[mask_row : mask_row + 1, :HALO].astype(F32) * jnp.where(inside, 1.0, 0.0),
        ],
        axis=1,
    )
    count = rows + 2 * HALO
    column = iota((rows, count), 1)
    near_first = jnp.where(odd == 1, -HALO, rows)
    far_first = jnp.where(odd == 1, rows, -HALO) - HALO - rows
    first = jnp.where(column < HALO, near_first, jnp.where(column < HALO + rows, -HALO, far_first))
    offset = column + first - iota((rows, count), 0)
    usable = (jnp.abs(offset) <= HALO) & ((mask > 0.5) | (offset == 0))
    scale = width ** (-0.5)
    for head in range(HEADS):
        columns = slice(head * width, (head + 1) * width)
        at, value_at = head * HALO, (HEADS + head) * HALO
        keys = jnp.concatenate(
            [near_ref[at : at + HALO, :], key_ref[0, :, columns], far_ref[at : at + HALO, :]], axis=0
        )
        values = jnp.concatenate(
            [
                near_ref[value_at : value_at + HALO, :],
                value_ref[0, :, columns],
                far_ref[value_at : value_at + HALO, :],
            ],
            axis=0,
        )
        scores = dot(query_ref[0, :, columns], keys, (1, 1)) * scale
        scores = jnp.where(usable, scores, NEG_FILL)
        raised = jnp.exp(scores - jnp.max(scores, axis=1, keepdims=True))
        soft = (raised * (1.0 / jnp.sum(raised, axis=1, keepdims=True))).astype(BF16)
        mixed_ref[:, columns] = (token_ref[0, :, columns].astype(F32) + dot(soft, values)).astype(BF16)
    pack(mixed_ref[...], place_ref, message_refs, pitch)


def far_part(refs, which):
    halves = [r.shape[0] // 2 for r in refs]
    return jnp.concatenate([r[which * n : (which + 1) * n, :] for r, n in zip(refs, halves, strict=True)], axis=0)


def expert_body(*refs):
    *row_refs, in_ref, out_ref, hidden_ref, partial_ref = refs
    rows = row_refs[0][...] if len(row_refs) == 1 else far_part(row_refs, 0)
    for at in range(0, in_ref.shape[1], STEP):
        hidden_ref[:, at : at + STEP] = jax.nn.gelu(dot(rows, in_ref[:, at : at + STEP])).astype(BF16)
    hidden = hidden_ref[...]
    for at in range(0, out_ref.shape[1], STEP):
        partial_ref[:, at : at + STEP] = dot(hidden, out_ref[:, at : at + STEP]).astype(BF16)


def finish_body(order, pitch, mixed_ref, back_ref, *refs):
    *message_refs, layer_ref = refs
    width = message_refs[0].shape[1]
    ordered = [message_refs[order.index(k)] for k in range(len(order))]
    for j, column in enumerate(from_messages(ordered, pitch, back_ref.shape[1])):
        columns = slice(j * width, (j + 1) * width)
        taken = dot(back_ref[...], column)
        layer_ref[0, :, columns] = (mixed_ref[:, columns].astype(F32) + taken).astype(BF16)


def half_terms(refs, side):
    hidden_refs, cot_refs = refs[:SPLIT], refs[SPLIT : 2 * SPLIT - 1]
    cot = jnp.concatenate([c[...] for c in cot_refs] + [far_part(refs[2 * SPLIT - 1 : 2 * SPLIT + 1], 1)], axis=0)
    half = hidden_refs[0].shape[1] // 2
    start = (lax.axis_index("grp") ^ side) * half
    for at in range(0, half, STEP):
        columns = pl.ds(pl.multiple_of(start + at, STEP), STEP)
        hidden = jnp.concatenate([h[:, columns] for h in hidden_refs], axis=0)
        yield at, dot(hidden, cot, (0, 0)).astype(BF16)


def other_half_body(*refs):
    piece_refs = refs[2 * SPLIT + 1 :]
    rows = piece_refs[0].shape[0]
    for at, term in half_terms(refs, 1):
        for r in range(0, STEP, rows):
            piece_refs[(at + r) // rows][...] = term[r : r + rows, :]


def own_half_body(*refs):
    *piece_refs, grad_ref, done_ref = refs[2 * SPLIT + 1 :]
    rows = piece_refs[0].shape[0]
    done_ref[...] = jnp.zeros_like(done_ref)
    for at, term in half_terms(refs, 0):
        for r in range(0, STEP, rows):
            theirs = piece_refs[(at + r) // rows][...].astype(F32)
            grad_ref[0, at + r : at + r + rows, :] = (term[r : r + rows, :].astype(F32) + theirs).astype(BF16)


def whole_term_body(*refs):
    hidden = jnp.concatenate([h[...] for h in refs[:SPLIT]], axis=0)
    cot = jnp.concatenate([c[...] for c in refs[SPLIT : 2 * SPLIT - 1]] + [far_part(refs[-3:-1], 1)], axis=0)
    refs[-1][...] = dot(hidden, cot, (0, 0)).astype(BF16)


def permute(value, apart):
    return lax.ppermute(value, "ep", [(i, i ^ apart) for i in range(lax.axis_size("ep"))])


def forward_body(first_row, rows_ref, cot_ref, both_ref):
    count = both_ref.shape[0] // 2
    both_ref[:count, :] = rows_ref[first_row : first_row + count, :]
    both_ref[count:, :] = cot_ref[first_row : first_row + count, :]


def forwarded(rows, cot, first_row, count, apart):
    (both,) = call(functools.partial(forward_body, first_row), [out(2 * count, rows.shape[1])], vmem=(rows, cot))
    return permute(both, apart)


def along_line(messages):
    return [m if k == 0 else permute(m, SPLIT * k) for k, m in enumerate(messages)]


def shards(tokens, queries, keys, values, key_mask, labels, cotangent, weight_in, weight_out):
    rows_here, features = tokens.shape[1:]
    axis_count = lax.axis_size("ep")
    experts = axis_count // SPLIT
    capacity = rows_here // experts + max(1, rows_here // (8 * experts))
    width = features // PARTS
    pitch = capacity + capacity % 2
    height = -(-PARTS * pitch // 16) * 16
    plane_rows = -(-experts * pitch // 16) * 16
    hidden_units = weight_in.shape[1]
    head_width = features // HEADS
    label_row = labels.reshape(1, rows_here)
    message = out(height, width)
    block = out(1, rows_here, features)
    row_ints = pltpu.VMEM((1, rows_here), jnp.int32)
    block_scratch = pltpu.VMEM((1, rows_here, features), BF16)

    halo = out(2 * HEADS * HALO + 16, head_width)
    near, far, key_here, value_here, mask_here = call(
        halo_body,
        (halo, halo, block, block, out(1, rows_here, dtype=jnp.int32)),
        hbm=(keys, values, key_mask),
        scratch=[pltpu.SemaphoreType.DMA((3,))],
    )
    near = permute(near, 1)
    steps = [(i, i + 1) for i in range(1, axis_count - 1, 2)]
    far = lax.ppermute(far, "ep", steps + [(j, i) for i, j in steps])

    place, place_back, query_here, token_here, *sent = call(
        functools.partial(pack_body, pitch),
        [out(plane_rows, rows_here), out(rows_here, plane_rows), block, block]
        + [message] * experts,
        hbm=(cotangent, label_row, queries, tokens),
        after=(key_here,),
        scratch=[block_scratch, row_ints, pltpu.SemaphoreType.DMA((4,))],
        size=0,
    )
    cot_got = along_line(sent)
    in_here, out_here = weight_in, weight_out.reshape(weight_out.shape[1:])

    mixed, *sent = call(
        functools.partial(attention_body, pitch),
        [out(rows_here, features)] + [message] * experts,
        vmem=(query_here, token_here, key_here, value_here, mask_here, near, far, place),
        flops=4 * rows_here * (rows_here + 2 * HALO) * features,
    )

    (cot_rows,) = call(
        functools.partial(gather_body, range(experts), pitch),
        [out(plane_rows, features)],
        vmem=cot_got,
        after=(mixed,),
        size=0,
    )
    cot_x, cot_y = permute(cot_rows, 1), permute(cot_rows, 2)
    mixed_got = along_line(sent)
    order = [0, *range(2, experts), 1]
    (rows,) = call(
        functools.partial(gather_body, order, pitch),
        [out(plane_rows, features)],
        vmem=[mixed_got[k] for k in order],
    )

    row_x, row_y = permute(rows, 1), permute(rows, 2)
    part = plane_rows // 32 * 16
    far = (forwarded(row_x, cot_x, 0, part, 2), forwarded(row_y, cot_y, part, plane_rows - part, 1))
    hiddens, partials = [], []
    for pieces, first in (((rows,), (cot_x, cot_y)), ((row_x,), ()), ((row_y,), ()), (far, ())):
        hidden, partial = call(
            expert_body,
            [out(plane_rows, hidden_units), out(plane_rows, features)],
            vmem=(*pieces, in_here, out_here),
            after=(*first, *hiddens[:1]),
            flops=4 * plane_rows * features * hidden_units,
        )
        hiddens.append(hidden)
        partials.append(partial)

    sums = [p if k == 0 else permute(p, k) for k, p in enumerate(partials)]

    inputs = (*hiddens, cot_rows, cot_x, cot_y, *far)
    flops = SPLIT * plane_rows * features * hidden_units
    if lax.axis_size("grp") == 2:
        half = hidden_units // 2
        pieces = call(
            other_half_body, [out(half // PIECES, features)] * PIECES, vmem=inputs, after=sums[1:3], flops=flops
        )
        theirs = [lax.ppermute(piece, "grp", [(0, 1), (1, 0)]) for piece in pieces]
        grad, done = call(
            own_half_body,
            [out(1, half, features), out(8, 128, dtype=F32)],
            vmem=(*inputs, *theirs),
            flops=flops,
        )
        ready = (done,)
    else:
        (term,) = call(whole_term_body, [out(hidden_units, features)], vmem=inputs, flops=2 * flops)
        grad = lax.psum_scatter(term, "grp", scatter_dimension=0, tiled=True)[None]
        ready = ()
    sent = call(functools.partial(combine_body, pitch), [message] * experts, vmem=sums)
    back = along_line(sent)
    order = [0, *range(experts - 1, 0, -1)]
    (layer_out,) = call(
        functools.partial(finish_body, order, pitch), [block], vmem=(mixed, place_back, *[back[k] for k in order]), after=ready
    )
    return (layer_out, grad)


def solution(mesh):
    in_specs = (
        P("grp", "ep", None),
        P("grp", "ep", None),
        P("grp", "ep", None),
        P("grp", "ep", None),
        P("grp", "ep"),
        P("grp", "ep", None),
        P("grp", "ep", None),
        P(None, "ep"),
        P("ep", None, None),
    )
    out_specs = (P("grp", "ep", None), P("ep", "grp", None))
    return jax.shard_map(shards, mesh=mesh, in_specs=in_specs, out_specs=out_specs, check_vma=False)
```

```python
import functools

import jax
import jax.numpy as jnp
from jax import lax
from jax.experimental import pallas as pl
from jax.experimental.pallas import tpu as pltpu
from jax.sharding import PartitionSpec as P

HEADS = 8
SPLIT = 4
HALO = 64
NEG_FILL = -1e30
PARTS = 4
STEP = 256
PIECES = 4
BF16 = jnp.bfloat16
F32 = jnp.float32
VMEM_LIMIT = 48 * 1024 * 1024
HBM = pl.BlockSpec(memory_space=pltpu.HBM)
VMEM = pl.BlockSpec(memory_space=pltpu.VMEM)
ANY = pl.BlockSpec(memory_space=pl.ANY)


def call(body, outs, vmem=(), hbm=(), after=(), scratch=(), flops=0, size=None):
    args = (*vmem, *(pltpu.with_memory_space_constraint(a, pltpu.HBM) for a in hbm), *after)
    n_in, n_after = len(vmem) + len(hbm), len(after)

    def kernel(*refs):
        body(*refs[:n_in], *refs[n_in + n_after :])

    if size is None:
        size = sum(a.size * a.dtype.itemsize for a in (*vmem, *hbm, *outs))
    return pl.pallas_call(
        kernel,
        out_shape=outs,
        in_specs=[VMEM] * len(vmem) + [HBM] * len(hbm) + [ANY] * n_after,
        out_specs=[VMEM] * len(outs),
        scratch_shapes=scratch,
        compiler_params=pltpu.CompilerParams(vmem_limit_bytes=VMEM_LIMIT),
        cost_estimate=pl.CostEstimate(flops=flops, bytes_accessed=size, transcendentals=0),
    )(*args)


def load(pairs, sems):
    copies = [pltpu.make_async_copy(src, dst, sems.at[i]) for i, (src, dst) in enumerate(pairs)]
    for c in copies:
        c.start()
    return copies


def dot(a, b, contract=(1, 0)):
    return lax.dot_general(
        a, b, (((contract[0],), (contract[1],)), ((), ())), preferred_element_type=F32
    )


def out(*shape, dtype=BF16):
    return jax.ShapeDtypeStruct(shape, dtype)


def iota(shape, dim):
    return lax.broadcasted_iota(jnp.int32, shape, dim)


def one_hot(condition):
    return jnp.where(condition, 1.0, 0.0).astype(BF16)


def column_blocks(rows):
    width = rows.shape[1] // PARTS
    return jnp.concatenate([rows[:, j * width : (j + 1) * width] for j in range(PARTS)], axis=0)


def home_plane():
    return lax.axis_index("ep") // SPLIT


def halo_body(key_hbm, value_hbm, mask_hbm, near_out, far_out, key_ref, value_ref, mask_ref, sems):
    copies = load(((key_hbm, key_ref), (value_hbm, value_ref), (mask_hbm, mask_ref)), sems)
    for c in copies:
        c.wait()
    rows = key_ref.shape[1]
    width = key_ref.shape[2] // HEADS
    odd = lax.axis_index("ep") % 2
    for message, last in ((near_out, 1 - odd), (far_out, odd)):
        mine = pl.ds(pl.multiple_of(last * (rows - HALO), HALO), HALO)
        for head in range(HEADS):
            columns = slice(head * width, (head + 1) * width)
            message[head * HALO : (head + 1) * HALO, :] = key_ref[0, mine, columns]
            start = (HEADS + head) * HALO
            message[start : start + HALO, :] = value_ref[0, mine, columns]
        mask = jnp.where(last == 1, mask_ref[:, rows - HALO :], mask_ref[:, :HALO]).astype(F32)
        mask = jnp.concatenate([mask, jnp.zeros((1, width - HALO), F32)], axis=1)
        message[2 * HEADS * HALO :, :] = jnp.broadcast_to(mask, (16, width)).astype(BF16)


def routed(labels):
    count = labels.shape[1]
    row, column = iota((count, count), 0), iota((count, count), 1)
    as_column = jnp.sum(jnp.where(row == column, labels, 0), axis=1, keepdims=True)
    same = as_column == labels
    slot = jnp.sum(jnp.where((row < column) & same, 1, 0), axis=0, keepdims=True)
    return as_column, slot, jnp.sum(jnp.where((column < row) & same, 1, 0), axis=1, keepdims=True)


def to_messages(rows, message_refs, pitch):
    height, width = message_refs[0].shape
    for p, message in enumerate(message_refs):
        for j in range(PARTS):
            start = j * (height // PARTS)
            message[start : start + pitch, :] = rows[p * pitch : (p + 1) * pitch, j * width : (j + 1) * width]


def from_messages(message_refs, pitch, height):
    step, width = message_refs[0].shape[0] // PARTS, message_refs[0].shape[1]
    columns = []
    for j in range(PARTS):
        blocks = [m[j * step : j * step + pitch, :] for m in message_refs]
        spare = height - pitch * len(blocks)
        columns.append(jnp.concatenate(blocks + [jnp.zeros((spare, width), BF16)] * (spare > 0), axis=0))
    return columns


def pack(rows, place_ref, message_refs, pitch):
    to_messages(dot(place_ref[...], rows).astype(BF16), message_refs, pitch)


def pack_body(pitch, cot_hbm, label_hbm, query_hbm, token_hbm, place_ref, back_ref, query_ref, token_ref, *refs):
    *message_refs, cot_ref, label_ref, sems = refs
    copies = load(
        ((label_hbm, label_ref), (cot_hbm, cot_ref), (query_hbm, query_ref), (token_hbm, token_ref)), sems
    )
    copies[0].wait()
    labels = label_ref[...]
    label_column, slot, slot_column = routed(labels)
    home = home_plane()
    place_ref[...] = one_hot((labels ^ home) * pitch + slot == iota(place_ref.shape, 0))
    back_ref[...] = one_hot((label_column ^ home) * pitch + slot_column == iota(back_ref.shape, 1))
    copies[1].wait()
    pack(cot_ref[0], place_ref, message_refs, pitch)
    for c in copies[2:]:
        c.wait()


def gather_body(pitch, *refs):
    *message_refs, rows_ref = refs
    width = message_refs[0].shape[1]
    for j, column in enumerate(from_messages(message_refs, pitch, rows_ref.shape[0])):
        rows_ref[:, j * width : (j + 1) * width] = column


def combine_body(pitch, *refs):
    partial_refs, message_refs = refs[:SPLIT], refs[SPLIT:]
    total = partial_refs[0][...].astype(F32)
    for partial_ref in partial_refs[1:]:
        total += partial_ref[...].astype(F32)
    to_messages(total.astype(BF16), message_refs, pitch)


def attention_body(
    pitch, query_ref, token_ref, key_ref, value_ref, mask_ref, near_ref, far_ref, place_ref, mixed_ref, *message_refs
):
    rows, features = query_ref.shape[1:]
    width = features // HEADS
    position = lax.axis_index("ep")
    odd = position % 2
    inside = (position > 0) & (position < lax.axis_size("ep") - 1)
    mask_row = 2 * HEADS * HALO
    mask = jnp.concatenate(
        [
            near_ref[mask_row : mask_row + 1, :HALO].astype(F32),
            mask_ref[...].astype(F32),
            far_ref[mask_row : mask_row + 1, :HALO].astype(F32) * jnp.where(inside, 1.0, 0.0),
        ],
        axis=1,
    )
    count = rows + 2 * HALO
    column = iota((rows, count), 1)
    near_first = jnp.where(odd == 1, -HALO, rows)
    far_first = jnp.where(odd == 1, rows, -HALO) - HALO - rows
    first = jnp.where(column < HALO, near_first, jnp.where(column < HALO + rows, -HALO, far_first))
    offset = column + first - iota((rows, count), 0)
    usable = (jnp.abs(offset) <= HALO) & ((mask > 0.5) | (offset == 0))
    scale = width ** (-0.5)
    for head in range(HEADS):
        columns = slice(head * width, (head + 1) * width)
        at, value_at = head * HALO, (HEADS + head) * HALO
        keys = jnp.concatenate(
            [near_ref[at : at + HALO, :], key_ref[0, :, columns], far_ref[at : at + HALO, :]], axis=0
        )
        values = jnp.concatenate(
            [
                near_ref[value_at : value_at + HALO, :],
                value_ref[0, :, columns],
                far_ref[value_at : value_at + HALO, :],
            ],
            axis=0,
        )
        scores = dot(query_ref[0, :, columns], keys, (1, 1)) * scale
        scores = jnp.where(usable, scores, NEG_FILL)
        raised = jnp.exp(scores - jnp.max(scores, axis=1, keepdims=True))
        soft = (raised * (1.0 / jnp.sum(raised, axis=1, keepdims=True))).astype(BF16)
        mixed_ref[:, columns] = (token_ref[0, :, columns].astype(F32) + dot(soft, values)).astype(BF16)
    pack(mixed_ref[...], place_ref, message_refs, pitch)


def far_part(refs, which):
    halves = [r.shape[0] // 2 for r in refs]
    return jnp.concatenate([r[which * n : (which + 1) * n, :] for r, n in zip(refs, halves, strict=True)], axis=0)


def expert_body(*refs):
    *row_refs, in_ref, out_ref, hidden_ref, partial_ref = refs
    rows = row_refs[0][...] if len(row_refs) == 1 else far_part(row_refs, 0)
    for at in range(0, in_ref.shape[1], STEP):
        hidden_ref[:, at : at + STEP] = jax.nn.gelu(dot(rows, in_ref[:, at : at + STEP])).astype(BF16)
    hidden = hidden_ref[...]
    for at in range(0, out_ref.shape[1], STEP):
        partial_ref[:, at : at + STEP] = dot(hidden, out_ref[:, at : at + STEP]).astype(BF16)


def finish_body(order, pitch, mixed_ref, back_ref, *refs):
    *message_refs, layer_ref = refs
    width = message_refs[0].shape[1]
    ordered = [message_refs[order.index(k)] for k in range(len(order))]
    for j, column in enumerate(from_messages(ordered, pitch, back_ref.shape[1])):
        columns = slice(j * width, (j + 1) * width)
        taken = dot(back_ref[...], column)
        layer_ref[0, :, columns] = (mixed_ref[:, columns].astype(F32) + taken).astype(BF16)


def half_terms(refs, side):
    hidden_refs, cot_refs = refs[:SPLIT], refs[SPLIT : 2 * SPLIT - 1]
    cot = jnp.concatenate([c[...] for c in cot_refs] + [far_part(refs[2 * SPLIT - 1 : 2 * SPLIT + 1], 1)], axis=0)
    half = hidden_refs[0].shape[1] // 2
    start = (lax.axis_index("grp") ^ side) * half
    for at in range(0, half, STEP):
        columns = pl.ds(pl.multiple_of(start + at, STEP), STEP)
        hidden = jnp.concatenate([h[:, columns] for h in hidden_refs], axis=0)
        yield at, dot(hidden, cot, (0, 0)).astype(BF16)


def other_half_body(*refs):
    piece_refs = refs[2 * SPLIT + 1 :]
    rows = piece_refs[0].shape[0]
    for at, term in half_terms(refs, 1):
        for r in range(0, STEP, rows):
            piece_refs[(at + r) // rows][...] = term[r : r + rows, :]


def own_half_body(*refs):
    *piece_refs, grad_ref, done_ref = refs[2 * SPLIT + 1 :]
    rows = piece_refs[0].shape[0]
    done_ref[...] = jnp.zeros_like(done_ref)
    for at, term in half_terms(refs, 0):
        for r in range(0, STEP, rows):
            theirs = piece_refs[(at + r) // rows][...].astype(F32)
            grad_ref[0, at + r : at + r + rows, :] = (term[r : r + rows, :].astype(F32) + theirs).astype(BF16)


def whole_term_body(*refs):
    hidden = jnp.concatenate([h[...] for h in refs[:SPLIT]], axis=0)
    cot = jnp.concatenate([c[...] for c in refs[SPLIT : 2 * SPLIT - 1]] + [far_part(refs[-3:-1], 1)], axis=0)
    refs[-1][...] = dot(hidden, cot, (0, 0)).astype(BF16)


def permute(value, apart):
    return lax.ppermute(value, "ep", [(i, i ^ apart) for i in range(lax.axis_size("ep"))])


def forward_body(first_row, rows_ref, cot_ref, both_ref):
    count = both_ref.shape[0] // 2
    both_ref[:count, :] = rows_ref[first_row : first_row + count, :]
    both_ref[count:, :] = cot_ref[first_row : first_row + count, :]


def forwarded(rows, cot, first_row, count, apart):
    (both,) = call(functools.partial(forward_body, first_row), [out(2 * count, rows.shape[1])], vmem=(rows, cot))
    return permute(both, apart)


def of_other_core(value):
    size = lax.axis_size("grp")
    return lax.ppermute(value[:16, :128], "grp", [(i, i ^ 1) for i in range(size)])


def along_line(messages):
    return [m if k == 0 else permute(m, SPLIT * k) for k, m in enumerate(messages)]


def shards(tokens, queries, keys, values, key_mask, labels, cotangent, weight_in, weight_out):
    rows_here, features = tokens.shape[1:]
    axis_count = lax.axis_size("ep")
    experts = axis_count // SPLIT
    capacity = rows_here // experts + max(1, rows_here // (8 * experts))
    width = features // PARTS
    pitch = capacity + capacity % 2
    height = -(-PARTS * pitch // 16) * 16
    plane_rows = -(-experts * pitch // 16) * 16
    hidden_units = weight_in.shape[1]
    head_width = features // HEADS
    label_row = labels.reshape(1, rows_here)
    message = out(height, width)
    block = out(1, rows_here, features)
    row_ints = pltpu.VMEM((1, rows_here), jnp.int32)
    block_scratch = pltpu.VMEM((1, rows_here, features), BF16)

    halo = out(2 * HEADS * HALO + 16, head_width)
    near, far, key_here, value_here, mask_here = call(
        halo_body,
        (halo, halo, block, block, out(1, rows_here, dtype=jnp.int32)),
        hbm=(keys, values, key_mask),
        scratch=[pltpu.SemaphoreType.DMA((3,))],
    )
    near = permute(near, 1)
    steps = [(i, i + 1) for i in range(1, axis_count - 1, 2)]
    far = lax.ppermute(far, "ep", steps + [(j, i) for i, j in steps])

    place, place_back, query_here, token_here, *sent = call(
        functools.partial(pack_body, pitch),
        [out(plane_rows, rows_here), out(rows_here, plane_rows), block, block]
        + [message] * experts,
        hbm=(cotangent, label_row, queries, tokens),
        after=(key_here,),
        scratch=[block_scratch, row_ints, pltpu.SemaphoreType.DMA((4,))],
        size=0,
    )
    cot_got = along_line(sent)
    in_here, out_here = weight_in, weight_out.reshape(weight_out.shape[1:])

    mixed, *sent = call(
        functools.partial(attention_body, pitch),
        [out(rows_here, features)] + [message] * experts,
        vmem=(query_here, token_here, key_here, value_here, mask_here, near, far, place),
        flops=4 * rows_here * (rows_here + 2 * HALO) * features,
    )

    (cot_rows,) = call(
        functools.partial(gather_body, pitch),
        [out(plane_rows, features)],
        vmem=cot_got,
        after=(mixed,),
        size=0,
    )
    cot_x, cot_y = permute(cot_rows, 1), permute(cot_rows, 2)
    (rows,) = call(functools.partial(gather_body, pitch), [out(plane_rows, features)], vmem=along_line(sent))

    row_x, row_y = permute(rows, 1), permute(rows, 2)
    part = plane_rows // 32 * 16
    far = (forwarded(row_x, cot_x, 0, part, 2), forwarded(row_y, cot_y, part, plane_rows - part, 1))
    hiddens, partials = [], []
    for pieces, first in (((rows,), (cot_x, cot_y)), ((row_x,), ()), ((row_y,), ()), (far, ())):
        hidden, partial = call(
            expert_body,
            [out(plane_rows, hidden_units), out(plane_rows, features)],
            vmem=(*pieces, in_here, out_here),
            after=(*first, *hiddens[:1], *[of_other_core(h) for h in hiddens[2:]]),
            flops=4 * plane_rows * features * hidden_units,
        )
        hiddens.append(hidden)
        partials.append(partial)

    sums = [p if k == 0 else permute(p, k) for k, p in enumerate(partials)]

    inputs = (*hiddens, cot_rows, cot_x, cot_y, *far)
    flops = SPLIT * plane_rows * features * hidden_units
    if lax.axis_size("grp") == 2:
        half = hidden_units // 2
        pieces = call(
            other_half_body, [out(half // PIECES, features)] * PIECES, vmem=inputs, after=sums[1:3], flops=flops
        )
        theirs = [lax.ppermute(piece, "grp", [(0, 1), (1, 0)]) for piece in pieces]
        grad, done = call(
            own_half_body,
            [out(1, half, features), out(8, 128, dtype=F32)],
            vmem=(*inputs, *theirs),
            flops=flops,
        )
        ready = (done,)
    else:
        (term,) = call(whole_term_body, [out(hidden_units, features)], vmem=inputs, flops=2 * flops)
        grad = lax.psum_scatter(term, "grp", scatter_dimension=0, tiled=True)[None]
        ready = ()
    sent = call(functools.partial(combine_body, pitch), [message] * experts, vmem=sums)
    back = along_line(sent)
    order = [0, *range(experts - 1, 0, -1)]
    (layer_out,) = call(
        functools.partial(finish_body, order, pitch), [block], vmem=(mixed, place_back, *[back[k] for k in order]), after=ready
    )
    return (layer_out, grad)


def solution(mesh):
    in_specs = (
        P("grp", "ep", None),
        P("grp", "ep", None),
        P("grp", "ep", None),
        P("grp", "ep", None),
        P("grp", "ep"),
        P("grp", "ep", None),
        P("grp", "ep", None),
        P(None, "ep"),
        P("ep", None, None),
    )
    out_specs = (P("grp", "ep", None), P("ep", "grp", None))
    return jax.shard_map(shards, mesh=mesh, in_specs=in_specs, out_specs=out_specs, check_vma=False)
```

```python
import functools

import jax
import jax.numpy as jnp
from jax import lax
from jax.experimental import pallas as pl
from jax.experimental.pallas import tpu as pltpu
from jax.sharding import PartitionSpec as P

HEADS = 8
SPLIT = 4
HALO = 64
NEG_FILL = -1e30
LOG2_E = 1.4426950408889634
PARTS = 4
STEP = 256
PIECES = 4
BF16 = jnp.bfloat16
F32 = jnp.float32
VMEM_LIMIT = 48 * 1024 * 1024
HBM = pl.BlockSpec(memory_space=pltpu.HBM)
VMEM = pl.BlockSpec(memory_space=pltpu.VMEM)
ANY = pl.BlockSpec(memory_space=pl.ANY)


def call(body, outs, vmem=(), hbm=(), after=(), scratch=(), flops=0, size=None):
    args = (*vmem, *(pltpu.with_memory_space_constraint(a, pltpu.HBM) for a in hbm), *after)
    n_in, n_after = len(vmem) + len(hbm), len(after)

    def kernel(*refs):
        body(*refs[:n_in], *refs[n_in + n_after :])

    if size is None:
        size = sum(a.size * a.dtype.itemsize for a in (*vmem, *hbm, *outs))
    return pl.pallas_call(
        kernel,
        out_shape=outs,
        in_specs=[VMEM] * len(vmem) + [HBM] * len(hbm) + [ANY] * n_after,
        out_specs=[VMEM] * len(outs),
        scratch_shapes=scratch,
        compiler_params=pltpu.CompilerParams(vmem_limit_bytes=VMEM_LIMIT),
        cost_estimate=pl.CostEstimate(flops=flops, bytes_accessed=size, transcendentals=0),
    )(*args)


def load(pairs, sems):
    copies = [pltpu.make_async_copy(src, dst, sems.at[i]) for i, (src, dst) in enumerate(pairs)]
    for c in copies:
        c.start()
    return copies


def dot(a, b, contract=(1, 0)):
    return lax.dot_general(
        a, b, (((contract[0],), (contract[1],)), ((), ())), preferred_element_type=F32
    )


def out(*shape, dtype=BF16):
    return jax.ShapeDtypeStruct(shape, dtype)


def iota(shape, dim):
    return lax.broadcasted_iota(jnp.int32, shape, dim)


def one_hot(condition):
    return jnp.where(condition, 1.0, 0.0).astype(BF16)


def column_blocks(rows):
    width = rows.shape[1] // PARTS
    return jnp.concatenate([rows[:, j * width : (j + 1) * width] for j in range(PARTS)], axis=0)


def home_plane():
    return lax.axis_index("ep") // SPLIT


def halo_body(key_hbm, value_hbm, mask_hbm, near_out, far_out, key_ref, value_ref, mask_ref, sems):
    copies = load(((key_hbm, key_ref), (value_hbm, value_ref), (mask_hbm, mask_ref)), sems)
    for c in copies:
        c.wait()
    rows = key_ref.shape[1]
    width = key_ref.shape[2] // HEADS
    odd = lax.axis_index("ep") % 2
    for parity in (0, 1):

        @pl.when(odd == parity)
        def _():
            for message, first in ((near_out, (1 - parity) * (rows - HALO)), (far_out, parity * (rows - HALO))):
                for head in range(HEADS):
                    columns = slice(head * width, (head + 1) * width)
                    message[head * HALO : (head + 1) * HALO, :] = key_ref[0, first : first + HALO, columns]
                    start = (HEADS + head) * HALO
                    message[start : start + HALO, :] = value_ref[0, first : first + HALO, columns]
                mask = mask_ref[:, first : first + HALO].astype(F32)
                mask = jnp.concatenate([mask, jnp.zeros((1, width - HALO), F32)], axis=1)
                message[2 * HEADS * HALO :, :] = jnp.broadcast_to(mask, (16, width)).astype(BF16)


def routed(labels):
    count = labels.shape[1]
    row, column = iota((count, count), 0), iota((count, count), 1)
    as_column = jnp.sum(jnp.where(row == column, labels, 0), axis=1, keepdims=True)
    same = as_column == labels
    slot = jnp.sum(jnp.where((row < column) & same, 1, 0), axis=0, keepdims=True)
    return as_column, slot, jnp.sum(jnp.where((column < row) & same, 1, 0), axis=1, keepdims=True)


def to_messages(rows, message_refs, pitch):
    height, width = message_refs[0].shape
    for p, message in enumerate(message_refs):
        for j in range(PARTS):
            start = j * (height // PARTS)
            message[start : start + pitch, :] = rows[p * pitch : (p + 1) * pitch, j * width : (j + 1) * width]


def from_messages(message_refs, pitch, height):
    step, width = message_refs[0].shape[0] // PARTS, message_refs[0].shape[1]
    columns = []
    for j in range(PARTS):
        blocks = [m[j * step : j * step + pitch, :] for m in message_refs]
        spare = height - pitch * len(blocks)
        columns.append(jnp.concatenate(blocks + [jnp.zeros((spare, width), BF16)] * (spare > 0), axis=0))
    return columns


def pack(rows, place_ref, message_refs, pitch):
    to_messages(dot(place_ref[...], rows).astype(BF16), message_refs, pitch)


def pack_body(pitch, cot_hbm, label_hbm, query_hbm, token_hbm, place_ref, back_ref, query_ref, token_ref, *refs):
    *message_refs, cot_ref, label_ref, sems = refs
    copies = load(
        ((label_hbm, label_ref), (cot_hbm, cot_ref), (query_hbm, query_ref), (token_hbm, token_ref)), sems
    )
    copies[0].wait()
    labels = label_ref[...]
    label_column, slot, slot_column = routed(labels)
    home = home_plane()
    place_ref[...] = one_hot((labels ^ home) * pitch + slot == iota(place_ref.shape, 0))
    back_ref[...] = one_hot((label_column ^ home) * pitch + slot_column == iota(back_ref.shape, 1))
    copies[1].wait()
    pack(cot_ref[0], place_ref, message_refs, pitch)
    for c in copies[2:]:
        c.wait()


def gather_body(order, pitch, *refs):
    *message_refs, rows_ref = refs
    width = message_refs[0].shape[1]
    ordered = [message_refs[order.index(k)] for k in range(len(order))]
    for j, column in enumerate(from_messages(ordered, pitch, rows_ref.shape[0])):
        rows_ref[:, j * width : (j + 1) * width] = column


def combine_body(pitch, *refs):
    partial_refs, message_refs = refs[:SPLIT], refs[SPLIT:]
    total = partial_refs[0][...].astype(F32)
    for partial_ref in partial_refs[1:]:
        total += partial_ref[...].astype(F32)
    to_messages(total.astype(BF16), message_refs, pitch)


def attention_body(
    pitch, query_ref, token_ref, key_ref, value_ref, mask_ref, near_ref, far_ref, place_ref, mixed_ref, *message_refs
):
    rows, features = query_ref.shape[1:]
    width = features // HEADS
    position = lax.axis_index("ep")
    odd = position % 2
    inside = (position > 0) & (position < lax.axis_size("ep") - 1)
    mask_row = 2 * HEADS * HALO
    mask = jnp.concatenate(
        [
            near_ref[mask_row : mask_row + 1, :HALO].astype(F32),
            mask_ref[...].astype(F32),
            far_ref[mask_row : mask_row + 1, :HALO].astype(F32) * jnp.where(inside, 1.0, 0.0),
        ],
        axis=1,
    )
    count = rows + 2 * HALO
    column = iota((rows, count), 1)
    near_first = jnp.where(odd == 1, -HALO, rows)
    far_first = jnp.where(odd == 1, rows, -HALO) - HALO - rows
    first = jnp.where(column < HALO, near_first, jnp.where(column < HALO + rows, -HALO, far_first))
    offset = column + first - iota((rows, count), 0)
    usable = (jnp.abs(offset) <= HALO) & ((mask > 0.5) | (offset == 0))
    factor = width ** (-0.5) * LOG2_E
    scored, valued, weighted = [], [], []
    for head in range(HEADS):
        columns = slice(head * width, (head + 1) * width)
        at, value_at = head * HALO, (HEADS + head) * HALO
        keys = [near_ref[at : at + HALO, :], key_ref[0, :, columns], far_ref[at : at + HALO, :]]
        values = [
            near_ref[value_at : value_at + HALO, :],
            value_ref[0, :, columns],
            far_ref[value_at : value_at + HALO, :],
        ]
        scored.append(dot(query_ref[0, :, columns], jnp.concatenate(keys, axis=0), (1, 1)))
        valued.append(jnp.concatenate(values, axis=0))
    for scores in scored:
        scores = jnp.where(usable, scores, NEG_FILL)
        raised = jnp.exp2((scores - jnp.max(scores, axis=1, keepdims=True)) * factor)
        weighted.append((raised.astype(BF16), 1.0 / jnp.sum(raised, axis=1, keepdims=True)))
    for head, (raised, share) in enumerate(weighted):
        columns = slice(head * width, (head + 1) * width)
        attended = dot(raised, valued[head]) * share
        mixed_ref[:, columns] = (token_ref[0, :, columns].astype(F32) + attended).astype(BF16)
    pack(mixed_ref[...], place_ref, message_refs, pitch)


def far_part(refs, which):
    halves = [r.shape[0] // 2 for r in refs]
    return jnp.concatenate([r[which * n : (which + 1) * n, :] for r, n in zip(refs, halves, strict=True)], axis=0)


def expert_body(*refs):
    *row_refs, in_ref, out_ref, hidden_ref, partial_ref = refs
    rows = row_refs[0][...] if len(row_refs) == 1 else far_part(row_refs, 0)
    for at in range(0, in_ref.shape[1], STEP):
        hidden_ref[:, at : at + STEP] = jax.nn.gelu(dot(rows, in_ref[:, at : at + STEP])).astype(BF16)
    hidden = hidden_ref[...]
    for at in range(0, out_ref.shape[1], STEP):
        partial_ref[:, at : at + STEP] = dot(hidden, out_ref[:, at : at + STEP]).astype(BF16)


def finish_body(order, pitch, mixed_ref, back_ref, *refs):
    *message_refs, layer_ref = refs
    width = message_refs[0].shape[1]
    ordered = [message_refs[order.index(k)] for k in range(len(order))]
    for j, column in enumerate(from_messages(ordered, pitch, back_ref.shape[1])):
        columns = slice(j * width, (j + 1) * width)
        taken = dot(back_ref[...], column)
        layer_ref[0, :, columns] = (mixed_ref[:, columns].astype(F32) + taken).astype(BF16)


def half_terms(refs, side):
    hidden_refs, cot_refs = refs[:SPLIT], refs[SPLIT : 2 * SPLIT - 1]
    cot = jnp.concatenate([c[...] for c in cot_refs] + [far_part(refs[2 * SPLIT - 1 : 2 * SPLIT + 1], 1)], axis=0)
    half = hidden_refs[0].shape[1] // 2
    start = (lax.axis_index("grp") ^ side) * half
    for at in range(0, half, STEP):
        columns = pl.ds(pl.multiple_of(start + at, STEP), STEP)
        hidden = jnp.concatenate([h[:, columns] for h in hidden_refs], axis=0)
        yield at, dot(hidden, cot, (0, 0)).astype(BF16)


def other_half_body(*refs):
    piece_refs = refs[2 * SPLIT + 1 :]
    rows = piece_refs[0].shape[0]
    for at, term in half_terms(refs, 1):
        for r in range(0, STEP, rows):
            piece_refs[(at + r) // rows][...] = term[r : r + rows, :]


def own_half_body(*refs):
    *piece_refs, grad_ref, done_ref = refs[2 * SPLIT + 1 :]
    rows = piece_refs[0].shape[0]
    done_ref[...] = jnp.zeros_like(done_ref)
    for at, term in half_terms(refs, 0):
        for r in range(0, STEP, rows):
            theirs = piece_refs[(at + r) // rows][...].astype(F32)
            grad_ref[0, at + r : at + r + rows, :] = (term[r : r + rows, :].astype(F32) + theirs).astype(BF16)


def whole_term_body(*refs):
    hidden = jnp.concatenate([h[...] for h in refs[:SPLIT]], axis=0)
    cot = jnp.concatenate([c[...] for c in refs[SPLIT : 2 * SPLIT - 1]] + [far_part(refs[-3:-1], 1)], axis=0)
    refs[-1][...] = dot(hidden, cot, (0, 0)).astype(BF16)


def permute(value, apart):
    return lax.ppermute(value, "ep", [(i, i ^ apart) for i in range(lax.axis_size("ep"))])


def forward_body(first_row, rows_ref, cot_ref, both_ref):
    count = both_ref.shape[0] // 2
    both_ref[:count, :] = rows_ref[first_row : first_row + count, :]
    both_ref[count:, :] = cot_ref[first_row : first_row + count, :]


def forwarded(rows, cot, first_row, count, apart):
    (both,) = call(functools.partial(forward_body, first_row), [out(2 * count, rows.shape[1])], vmem=(rows, cot))
    return permute(both, apart)


def of_other_core(value):
    size = lax.axis_size("grp")
    return lax.ppermute(value[:16, :128], "grp", [(i, i ^ 1) for i in range(size)])


def along_line(messages):
    return [m if k == 0 else permute(m, SPLIT * k) for k, m in enumerate(messages)]


def shards(tokens, queries, keys, values, key_mask, labels, cotangent, weight_in, weight_out):
    rows_here, features = tokens.shape[1:]
    axis_count = lax.axis_size("ep")
    experts = axis_count // SPLIT
    capacity = rows_here // experts + max(1, rows_here // (8 * experts))
    width = features // PARTS
    pitch = capacity + capacity % 2
    height = -(-PARTS * pitch // 16) * 16
    plane_rows = -(-experts * pitch // 16) * 16
    hidden_units = weight_in.shape[1]
    head_width = features // HEADS
    label_row = labels.reshape(1, rows_here)
    message = out(height, width)
    block = out(1, rows_here, features)
    row_ints = pltpu.VMEM((1, rows_here), jnp.int32)
    block_scratch = pltpu.VMEM((1, rows_here, features), BF16)

    halo = out(2 * HEADS * HALO + 16, head_width)
    near, far, key_here, value_here, mask_here = call(
        halo_body,
        (halo, halo, block, block, out(1, rows_here, dtype=jnp.int32)),
        hbm=(keys, values, key_mask),
        scratch=[pltpu.SemaphoreType.DMA((3,))],
    )
    near = permute(near, 1)
    steps = [(i, i + 1) for i in range(1, axis_count - 1, 2)]
    far = lax.ppermute(far, "ep", steps + [(j, i) for i, j in steps])

    place, place_back, query_here, token_here, *sent = call(
        functools.partial(pack_body, pitch),
        [out(plane_rows, rows_here), out(rows_here, plane_rows), block, block]
        + [message] * experts,
        hbm=(cotangent, label_row, queries, tokens),
        after=(key_here,),
        scratch=[block_scratch, row_ints, pltpu.SemaphoreType.DMA((4,))],
        size=0,
    )
    cot_got = along_line(sent)
    in_here, out_here = weight_in, weight_out.reshape(weight_out.shape[1:])

    mixed, *sent = call(
        functools.partial(attention_body, pitch),
        [out(rows_here, features)] + [message] * experts,
        vmem=(query_here, token_here, key_here, value_here, mask_here, near, far, place),
        flops=4 * rows_here * (rows_here + 2 * HALO) * features,
    )

    order = [0, 2, 1, *range(3, experts)]
    (cot_rows,) = call(
        functools.partial(gather_body, order, pitch),
        [out(plane_rows, features)],
        vmem=[cot_got[k] for k in order],
        after=(mixed,),
        size=0,
    )
    cot_x, cot_y = permute(cot_rows, 1), permute(cot_rows, 2)
    (rows,) = call(
        functools.partial(gather_body, range(experts), pitch), [out(plane_rows, features)], vmem=along_line(sent)
    )

    row_x, row_y = permute(rows, 1), permute(rows, 2)
    part = plane_rows // 32 * 16
    far = (forwarded(row_x, cot_x, 0, part, 2), forwarded(row_y, cot_y, part, plane_rows - part, 1))
    hiddens, partials = [], []
    for pieces, first in (((rows,), (cot_x, cot_y)), ((row_x,), ()), ((row_y,), ()), (far, ())):
        hidden, partial = call(
            expert_body,
            [out(plane_rows, hidden_units), out(plane_rows, features)],
            vmem=(*pieces, in_here, out_here),
            after=(*first, *hiddens[:1], *[of_other_core(h) for h in hiddens[2:]]),
            flops=4 * plane_rows * features * hidden_units,
        )
        hiddens.append(hidden)
        partials.append(partial)

    sums = [p if k == 0 else permute(p, k) for k, p in enumerate(partials)]

    inputs = (*hiddens, cot_rows, cot_x, cot_y, *far)
    flops = SPLIT * plane_rows * features * hidden_units
    if lax.axis_size("grp") == 2:
        half = hidden_units // 2
        pieces = call(
            other_half_body, [out(half // PIECES, features)] * PIECES, vmem=inputs, after=sums[1:3], flops=flops
        )
        theirs = [lax.ppermute(piece, "grp", [(0, 1), (1, 0)]) for piece in pieces]
        grad, done = call(
            own_half_body,
            [out(1, half, features), out(8, 128, dtype=F32)],
            vmem=(*inputs, *theirs),
            flops=flops,
        )
        ready = (done,)
    else:
        (term,) = call(whole_term_body, [out(hidden_units, features)], vmem=inputs, flops=2 * flops)
        grad = lax.psum_scatter(term, "grp", scatter_dimension=0, tiled=True)[None]
        ready = ()
    sent = call(functools.partial(combine_body, pitch), [message] * experts, vmem=sums)
    back = along_line(sent)
    order = [0, *range(experts - 1, 0, -1)]
    (layer_out,) = call(
        functools.partial(finish_body, order, pitch), [block], vmem=(mixed, place_back, *[back[k] for k in order]), after=ready
    )
    return (layer_out, grad)


def solution(mesh):
    in_specs = (
        P("grp", "ep", None),
        P("grp", "ep", None),
        P("grp", "ep", None),
        P("grp", "ep", None),
        P("grp", "ep"),
        P("grp", "ep", None),
        P("grp", "ep", None),
        P(None, "ep"),
        P("ep", None, None),
    )
    out_specs = (P("grp", "ep", None), P("ep", "grp", None))
    return jax.shard_map(shards, mesh=mesh, in_specs=in_specs, out_specs=out_specs, check_vma=False)
```

```python
import functools

import jax
import jax.numpy as jnp
from jax import lax
from jax.experimental import pallas as pl
from jax.experimental.pallas import tpu as pltpu
from jax.sharding import PartitionSpec as P

HEADS = 8
SPLIT = 4
HALO = 64
NEG_FILL = -1e30
LOG2_E = 1.4426950408889634
PARTS = 4
STEP = 256
PIECES = 4
BF16 = jnp.bfloat16
F32 = jnp.float32
VMEM_LIMIT = 48 * 1024 * 1024
HBM = pl.BlockSpec(memory_space=pltpu.HBM)
VMEM = pl.BlockSpec(memory_space=pltpu.VMEM)
ANY = pl.BlockSpec(memory_space=pl.ANY)


def call(body, outs, vmem=(), hbm=(), after=(), scratch=(), flops=0, size=None):
    args = (*vmem, *(pltpu.with_memory_space_constraint(a, pltpu.HBM) for a in hbm), *after)
    n_in, n_after = len(vmem) + len(hbm), len(after)

    def kernel(*refs):
        body(*refs[:n_in], *refs[n_in + n_after :])

    if size is None:
        size = sum(a.size * a.dtype.itemsize for a in (*vmem, *hbm, *outs))
    return pl.pallas_call(
        kernel,
        out_shape=outs,
        in_specs=[VMEM] * len(vmem) + [HBM] * len(hbm) + [ANY] * n_after,
        out_specs=[VMEM] * len(outs),
        scratch_shapes=scratch,
        compiler_params=pltpu.CompilerParams(vmem_limit_bytes=VMEM_LIMIT),
        cost_estimate=pl.CostEstimate(flops=flops, bytes_accessed=size, transcendentals=0),
    )(*args)


def load(pairs, sems):
    copies = [pltpu.make_async_copy(src, dst, sems.at[i]) for i, (src, dst) in enumerate(pairs)]
    for c in copies:
        c.start()
    return copies


def dot(a, b, contract=(1, 0)):
    return lax.dot_general(
        a, b, (((contract[0],), (contract[1],)), ((), ())), preferred_element_type=F32
    )


def out(*shape, dtype=BF16):
    return jax.ShapeDtypeStruct(shape, dtype)


def iota(shape, dim):
    return lax.broadcasted_iota(jnp.int32, shape, dim)


def one_hot(condition):
    return jnp.where(condition, 1.0, 0.0).astype(BF16)


def column_blocks(rows):
    width = rows.shape[1] // PARTS
    return jnp.concatenate([rows[:, j * width : (j + 1) * width] for j in range(PARTS)], axis=0)


def home_plane():
    return lax.axis_index("ep") // SPLIT


def halo_body(key_hbm, value_hbm, mask_hbm, near_out, far_out, key_ref, value_ref, mask_ref, sems):
    copies = load(((key_hbm, key_ref), (value_hbm, value_ref), (mask_hbm, mask_ref)), sems)
    for c in copies:
        c.wait()
    rows = key_ref.shape[1]
    width = key_ref.shape[2] // HEADS
    odd = lax.axis_index("ep") % 2
    for parity in (0, 1):

        @pl.when(odd == parity)
        def _():
            for message, first in ((near_out, (1 - parity) * (rows - HALO)), (far_out, parity * (rows - HALO))):
                for head in range(HEADS):
                    columns = slice(head * width, (head + 1) * width)
                    message[head * HALO : (head + 1) * HALO, :] = key_ref[0, first : first + HALO, columns]
                    start = (HEADS + head) * HALO
                    message[start : start + HALO, :] = value_ref[0, first : first + HALO, columns]
                mask = mask_ref[:, first : first + HALO].astype(F32)
                mask = jnp.concatenate([mask, jnp.zeros((1, width - HALO), F32)], axis=1)
                message[2 * HEADS * HALO :, :] = jnp.broadcast_to(mask, (16, width)).astype(BF16)


def routed(labels):
    count = labels.shape[1]
    row, column = iota((count, count), 0), iota((count, count), 1)
    as_column = jnp.sum(jnp.where(row == column, labels, 0), axis=1, keepdims=True)
    same = as_column == labels
    slot = jnp.sum(jnp.where((row < column) & same, 1, 0), axis=0, keepdims=True)
    return as_column, slot, jnp.sum(jnp.where((column < row) & same, 1, 0), axis=1, keepdims=True)


def to_messages(rows, message_refs, pitch):
    height, width = message_refs[0].shape
    for p, message in enumerate(message_refs):
        for j in range(PARTS):
            start = j * (height // PARTS)
            message[start : start + pitch, :] = rows[p * pitch : (p + 1) * pitch, j * width : (j + 1) * width]


def from_messages(message_refs, pitch, height):
    step, width = message_refs[0].shape[0] // PARTS, message_refs[0].shape[1]
    columns = []
    for j in range(PARTS):
        blocks = [m[j * step : j * step + pitch, :] for m in message_refs]
        spare = height - pitch * len(blocks)
        columns.append(jnp.concatenate(blocks + [jnp.zeros((spare, width), BF16)] * (spare > 0), axis=0))
    return columns


def pack(rows, place_ref, message_refs, pitch):
    to_messages(dot(place_ref[...], rows).astype(BF16), message_refs, pitch)


def pack_body(pitch, cot_hbm, label_hbm, query_hbm, token_hbm, place_ref, back_ref, query_ref, token_ref, *refs):
    *message_refs, cot_ref, label_ref, sems = refs
    copies = load(
        ((label_hbm, label_ref), (cot_hbm, cot_ref), (query_hbm, query_ref), (token_hbm, token_ref)), sems
    )
    copies[0].wait()
    labels = label_ref[...]
    label_column, slot, slot_column = routed(labels)
    home = home_plane()
    place_ref[...] = one_hot((labels ^ home) * pitch + slot == iota(place_ref.shape, 0))
    back_ref[...] = one_hot((label_column ^ home) * pitch + slot_column == iota(back_ref.shape, 1))
    copies[1].wait()
    pack(cot_ref[0], place_ref, message_refs, pitch)
    for c in copies[2:]:
        c.wait()


def gather_body(order, pitch, *refs):
    *message_refs, rows_ref = refs
    width = message_refs[0].shape[1]
    ordered = [message_refs[order.index(k)] for k in range(len(order))]
    for j, column in enumerate(from_messages(ordered, pitch, rows_ref.shape[0])):
        rows_ref[:, j * width : (j + 1) * width] = column


def combine_body(pitch, *refs):
    partial_refs, message_refs = refs[:SPLIT], refs[SPLIT:]
    total = partial_refs[0][...].astype(F32)
    for partial_ref in partial_refs[1:]:
        total += partial_ref[...].astype(F32)
    to_messages(total.astype(BF16), message_refs, pitch)


def attention_body(
    pitch, query_ref, token_ref, key_ref, value_ref, mask_ref, near_ref, far_ref, place_ref, mixed_ref, *message_refs
):
    rows, features = query_ref.shape[1:]
    width = features // HEADS
    position = lax.axis_index("ep")
    odd = position % 2
    inside = (position > 0) & (position < lax.axis_size("ep") - 1)
    mask_row = 2 * HEADS * HALO
    mask = jnp.concatenate(
        [
            near_ref[mask_row : mask_row + 1, :HALO].astype(F32),
            mask_ref[...].astype(F32),
            far_ref[mask_row : mask_row + 1, :HALO].astype(F32) * jnp.where(inside, 1.0, 0.0),
        ],
        axis=1,
    )
    count = rows + 2 * HALO
    column = iota((rows, count), 1)
    near_first = jnp.where(odd == 1, -HALO, rows)
    far_first = jnp.where(odd == 1, rows, -HALO) - HALO - rows
    first = jnp.where(column < HALO, near_first, jnp.where(column < HALO + rows, -HALO, far_first))
    offset = column + first - iota((rows, count), 0)
    usable = (jnp.abs(offset) <= HALO) & ((mask > 0.5) | (offset == 0))
    factor = width ** (-0.5) * LOG2_E
    scored, valued, weighted = [], [], []
    for head in range(HEADS):
        columns = slice(head * width, (head + 1) * width)
        at, value_at = head * HALO, (HEADS + head) * HALO
        keys = [near_ref[at : at + HALO, :], key_ref[0, :, columns], far_ref[at : at + HALO, :]]
        values = [
            near_ref[value_at : value_at + HALO, :],
            value_ref[0, :, columns],
            far_ref[value_at : value_at + HALO, :],
        ]
        scored.append(dot(query_ref[0, :, columns], jnp.concatenate(keys, axis=0), (1, 1)))
        valued.append(jnp.concatenate(values, axis=0))
    for scores in scored:
        scores = jnp.where(usable, scores, NEG_FILL)
        raised = jnp.exp2((scores - jnp.max(scores, axis=1, keepdims=True)) * factor)
        weighted.append((raised.astype(BF16), 1.0 / jnp.sum(raised, axis=1, keepdims=True)))
    for head, (raised, share) in enumerate(weighted):
        columns = slice(head * width, (head + 1) * width)
        attended = dot(raised, valued[head]) * share
        mixed_ref[:, columns] = (token_ref[0, :, columns].astype(F32) + attended).astype(BF16)
    pack(mixed_ref[...], place_ref, message_refs, pitch)


def far_part(refs, which):
    halves = [r.shape[0] // 2 for r in refs]
    return jnp.concatenate([r[which * n : (which + 1) * n, :] for r, n in zip(refs, halves, strict=True)], axis=0)


def expert_body(*refs):
    *row_refs, in_ref, out_ref, hidden_ref, partial_ref = refs
    rows = row_refs[0][...] if len(row_refs) == 1 else far_part(row_refs, 0)
    for at in range(0, in_ref.shape[1], STEP):
        hidden_ref[:, at : at + STEP] = jax.nn.gelu(dot(rows, in_ref[:, at : at + STEP])).astype(BF16)
    hidden = hidden_ref[...]
    for at in range(0, out_ref.shape[1], STEP):
        partial_ref[:, at : at + STEP] = dot(hidden, out_ref[:, at : at + STEP]).astype(BF16)


def finish_body(order, pitch, mixed_ref, back_ref, *refs):
    *message_refs, layer_ref = refs
    width = message_refs[0].shape[1]
    ordered = [message_refs[order.index(k)] for k in range(len(order))]
    taken = dot(back_ref[...], jnp.concatenate(from_messages(ordered, pitch, back_ref.shape[1]), axis=1))
    layer_ref[0, :, :] = (mixed_ref[...].astype(F32) + taken).astype(BF16)


def half_terms(refs, side):
    hidden_refs, cot_refs = refs[:SPLIT], refs[SPLIT : 2 * SPLIT - 1]
    cot = jnp.concatenate([c[...] for c in cot_refs] + [far_part(refs[2 * SPLIT - 1 : 2 * SPLIT + 1], 1)], axis=0)
    half = hidden_refs[0].shape[1] // 2
    start = (lax.axis_index("grp") ^ side) * half
    for at in range(0, half, STEP):
        columns = pl.ds(pl.multiple_of(start + at, STEP), STEP)
        hidden = jnp.concatenate([h[:, columns] for h in hidden_refs], axis=0)
        yield at, dot(hidden, cot, (0, 0)).astype(BF16)


def other_half_body(*refs):
    piece_refs = refs[2 * SPLIT + 1 :]
    rows = piece_refs[0].shape[0]
    for at, term in half_terms(refs, 1):
        for r in range(0, STEP, rows):
            piece_refs[(at + r) // rows][...] = term[r : r + rows, :]


def own_half_body(*refs):
    *piece_refs, grad_ref, done_ref = refs[2 * SPLIT + 1 :]
    rows = piece_refs[0].shape[0]
    done_ref[...] = jnp.zeros_like(done_ref)
    for at, term in half_terms(refs, 0):
        for r in range(0, STEP, rows):
            theirs = piece_refs[(at + r) // rows][...].astype(F32)
            grad_ref[0, at + r : at + r + rows, :] = (term[r : r + rows, :].astype(F32) + theirs).astype(BF16)


def whole_term_body(*refs):
    hidden = jnp.concatenate([h[...] for h in refs[:SPLIT]], axis=0)
    cot = jnp.concatenate([c[...] for c in refs[SPLIT : 2 * SPLIT - 1]] + [far_part(refs[-3:-1], 1)], axis=0)
    refs[-1][...] = dot(hidden, cot, (0, 0)).astype(BF16)


def permute(value, apart):
    return lax.ppermute(value, "ep", [(i, i ^ apart) for i in range(lax.axis_size("ep"))])


def forward_body(first_row, rows_ref, cot_ref, both_ref):
    count = both_ref.shape[0] // 2
    both_ref[:count, :] = rows_ref[first_row : first_row + count, :]
    both_ref[count:, :] = cot_ref[first_row : first_row + count, :]


def forwarded(rows, cot, first_row, count, apart):
    (both,) = call(functools.partial(forward_body, first_row), [out(2 * count, rows.shape[1])], vmem=(rows, cot))
    return permute(both, apart)


def of_other_core(value):
    size = lax.axis_size("grp")
    return lax.ppermute(value[:16, :128], "grp", [(i, i ^ 1) for i in range(size)])


def along_line(messages):
    return [m if k == 0 else permute(m, SPLIT * k) for k, m in enumerate(messages)]


def shards(tokens, queries, keys, values, key_mask, labels, cotangent, weight_in, weight_out):
    rows_here, features = tokens.shape[1:]
    axis_count = lax.axis_size("ep")
    experts = axis_count // SPLIT
    capacity = rows_here // experts + max(1, rows_here // (8 * experts))
    width = features // PARTS
    pitch = capacity + capacity % 2
    height = -(-PARTS * pitch // 16) * 16
    plane_rows = -(-experts * pitch // 16) * 16
    hidden_units = weight_in.shape[1]
    head_width = features // HEADS
    label_row = labels.reshape(1, rows_here)
    message = out(height, width)
    block = out(1, rows_here, features)
    row_ints = pltpu.VMEM((1, rows_here), jnp.int32)
    block_scratch = pltpu.VMEM((1, rows_here, features), BF16)

    halo = out(2 * HEADS * HALO + 16, head_width)
    near, far, key_here, value_here, mask_here = call(
        halo_body,
        (halo, halo, block, block, out(1, rows_here, dtype=jnp.int32)),
        hbm=(keys, values, key_mask),
        scratch=[pltpu.SemaphoreType.DMA((3,))],
    )
    near = permute(near, 1)
    steps = [(i, i + 1) for i in range(1, axis_count - 1, 2)]
    far = lax.ppermute(far, "ep", steps + [(j, i) for i, j in steps])

    place, place_back, query_here, token_here, *sent = call(
        functools.partial(pack_body, pitch),
        [out(plane_rows, rows_here), out(rows_here, plane_rows), block, block]
        + [message] * experts,
        hbm=(cotangent, label_row, queries, tokens),
        after=(key_here,),
        scratch=[block_scratch, row_ints, pltpu.SemaphoreType.DMA((4,))],
        size=0,
    )
    cot_got = along_line(sent)
    in_here, out_here = weight_in, weight_out.reshape(weight_out.shape[1:])

    mixed, *sent = call(
        functools.partial(attention_body, pitch),
        [out(rows_here, features)] + [message] * experts,
        vmem=(query_here, token_here, key_here, value_here, mask_here, near, far, place),
        flops=4 * rows_here * (rows_here + 2 * HALO) * features,
    )

    order = [0, 2, 1, *range(3, experts)]
    (cot_rows,) = call(
        functools.partial(gather_body, order, pitch),
        [out(plane_rows, features)],
        vmem=[cot_got[k] for k in order],
        after=(mixed,),
        size=0,
    )
    cot_x, cot_y = permute(cot_rows, 1), permute(cot_rows, 2)
    (rows,) = call(
        functools.partial(gather_body, range(experts), pitch), [out(plane_rows, features)], vmem=along_line(sent)
    )

    row_x, row_y = permute(rows, 1), permute(rows, 2)
    part = plane_rows // 32 * 16
    far = (forwarded(row_x, cot_x, 0, part, 2), forwarded(row_y, cot_y, part, plane_rows - part, 1))
    hiddens, partials = [], []
    for pieces, first in (((rows,), (cot_x, cot_y)), ((row_x,), ()), ((row_y,), ()), (far, ())):
        hidden, partial = call(
            expert_body,
            [out(plane_rows, hidden_units), out(plane_rows, features)],
            vmem=(*pieces, in_here, out_here),
            after=(*first, *hiddens[:1], *[of_other_core(h) for h in hiddens[2:]]),
            flops=4 * plane_rows * features * hidden_units,
        )
        hiddens.append(hidden)
        partials.append(partial)

    sums = [p if k == 0 else permute(p, k) for k, p in enumerate(partials)]

    inputs = (*hiddens, cot_rows, cot_x, cot_y, *far)
    flops = SPLIT * plane_rows * features * hidden_units
    if lax.axis_size("grp") == 2:
        half = hidden_units // 2
        pieces = call(
            other_half_body, [out(half // PIECES, features)] * PIECES, vmem=inputs, after=sums[1:3], flops=flops
        )
        theirs = [lax.ppermute(piece, "grp", [(0, 1), (1, 0)]) for piece in pieces]
        grad, done = call(
            own_half_body,
            [out(1, half, features), out(8, 128, dtype=F32)],
            vmem=(*inputs, *theirs),
            flops=flops,
        )
        ready = (done,)
    else:
        (term,) = call(whole_term_body, [out(hidden_units, features)], vmem=inputs, flops=2 * flops)
        grad = lax.psum_scatter(term, "grp", scatter_dimension=0, tiled=True)[None]
        ready = ()
    sent = call(functools.partial(combine_body, pitch), [message] * experts, vmem=sums)
    back = along_line(sent)
    order = [0, *range(experts - 1, 0, -1)]
    (layer_out,) = call(
        functools.partial(finish_body, order, pitch), [block], vmem=(mixed, place_back, *[back[k] for k in order]), after=ready
    )
    return (layer_out, grad)


def solution(mesh):
    in_specs = (
        P("grp", "ep", None),
        P("grp", "ep", None),
        P("grp", "ep", None),
        P("grp", "ep", None),
        P("grp", "ep"),
        P("grp", "ep", None),
        P("grp", "ep", None),
        P(None, "ep"),
        P("ep", None, None),
    )
    out_specs = (P("grp", "ep", None), P("ep", "grp", None))
    return jax.shard_map(shards, mesh=mesh, in_specs=in_specs, out_specs=out_specs, check_vma=False)
```

```python
import functools

import jax
import jax.numpy as jnp
from jax import lax
from jax.experimental import pallas as pl
from jax.experimental.pallas import tpu as pltpu
from jax.sharding import PartitionSpec as P

HEADS = 8
SPLIT = 4
HALO = 64
NEG_FILL = -1e30
LOG2_E = 1.4426950408889634
PARTS = 4
STEP = 256
PIECES = 4
BF16 = jnp.bfloat16
F32 = jnp.float32
VMEM_LIMIT = 48 * 1024 * 1024
HBM = pl.BlockSpec(memory_space=pltpu.HBM)
VMEM = pl.BlockSpec(memory_space=pltpu.VMEM)
ANY = pl.BlockSpec(memory_space=pl.ANY)


def call(body, outs, vmem=(), hbm=(), after=(), scratch=(), flops=0, size=None):
    args = (*vmem, *(pltpu.with_memory_space_constraint(a, pltpu.HBM) for a in hbm), *after)
    n_in, n_after = len(vmem) + len(hbm), len(after)

    def kernel(*refs):
        body(*refs[:n_in], *refs[n_in + n_after :])

    if size is None:
        size = sum(a.size * a.dtype.itemsize for a in (*vmem, *hbm, *outs))
    return pl.pallas_call(
        kernel,
        out_shape=outs,
        in_specs=[VMEM] * len(vmem) + [HBM] * len(hbm) + [ANY] * n_after,
        out_specs=[VMEM] * len(outs),
        scratch_shapes=scratch,
        compiler_params=pltpu.CompilerParams(vmem_limit_bytes=VMEM_LIMIT),
        cost_estimate=pl.CostEstimate(flops=flops, bytes_accessed=size, transcendentals=0),
    )(*args)


def load(pairs, sems):
    copies = [pltpu.make_async_copy(src, dst, sems.at[i]) for i, (src, dst) in enumerate(pairs)]
    for c in copies:
        c.start()
    return copies


def dot(a, b, contract=(1, 0)):
    return lax.dot_general(
        a, b, (((contract[0],), (contract[1],)), ((), ())), preferred_element_type=F32
    )


def out(*shape, dtype=BF16):
    return jax.ShapeDtypeStruct(shape, dtype)


def iota(shape, dim):
    return lax.broadcasted_iota(jnp.int32, shape, dim)


def one_hot(condition):
    return jnp.where(condition, 1.0, 0.0).astype(BF16)


def column_blocks(rows):
    width = rows.shape[1] // PARTS
    return jnp.concatenate([rows[:, j * width : (j + 1) * width] for j in range(PARTS)], axis=0)


def home_plane():
    return lax.axis_index("ep") // SPLIT


def halo_body(key_hbm, value_hbm, mask_hbm, near_out, far_out, key_ref, value_ref, mask_ref, sems):
    copies = load(((key_hbm, key_ref), (value_hbm, value_ref), (mask_hbm, mask_ref)), sems)
    for c in copies:
        c.wait()
    rows = key_ref.shape[1]
    width = key_ref.shape[2] // HEADS
    odd = lax.axis_index("ep") % 2
    for parity in (0, 1):

        @pl.when(odd == parity)
        def _():
            for message, first in ((near_out, (1 - parity) * (rows - HALO)), (far_out, parity * (rows - HALO))):
                for head in range(HEADS):
                    columns = slice(head * width, (head + 1) * width)
                    message[head * HALO : (head + 1) * HALO, :] = key_ref[0, first : first + HALO, columns]
                    start = (HEADS + head) * HALO
                    message[start : start + HALO, :] = value_ref[0, first : first + HALO, columns]
                mask = mask_ref[:, first : first + HALO].astype(F32)
                mask = jnp.concatenate([mask, jnp.zeros((1, width - HALO), F32)], axis=1)
                message[2 * HEADS * HALO :, :] = jnp.broadcast_to(mask, (16, width)).astype(BF16)


def routed(labels):
    count = labels.shape[1]
    row, column = iota((count, count), 0), iota((count, count), 1)
    as_column = jnp.sum(jnp.where(row == column, labels, 0), axis=1, keepdims=True)
    same = as_column == labels
    slot = jnp.sum(jnp.where((row < column) & same, 1, 0), axis=0, keepdims=True)
    return as_column, slot, jnp.sum(jnp.where((column < row) & same, 1, 0), axis=1, keepdims=True)


def to_messages(rows, message_refs, pitch):
    height, width = message_refs[0].shape
    for p, message in enumerate(message_refs):
        for j in range(PARTS):
            start = j * (height // PARTS)
            message[start : start + pitch, :] = rows[p * pitch : (p + 1) * pitch, j * width : (j + 1) * width]


def from_messages(message_refs, pitch, height):
    step, width = message_refs[0].shape[0] // PARTS, message_refs[0].shape[1]
    columns = []
    for j in range(PARTS):
        blocks = [m[j * step : j * step + pitch, :] for m in message_refs]
        spare = height - pitch * len(blocks)
        columns.append(jnp.concatenate(blocks + [jnp.zeros((spare, width), BF16)] * (spare > 0), axis=0))
    return columns


def pack(rows, place_ref, message_refs, pitch):
    to_messages(dot(place_ref[...], rows).astype(BF16), message_refs, pitch)


def pack_body(pitch, cot_hbm, label_hbm, query_hbm, token_hbm, place_ref, back_ref, query_ref, token_ref, *refs):
    *message_refs, cot_ref, label_ref, sems = refs
    copies = load(
        ((label_hbm, label_ref), (cot_hbm, cot_ref), (query_hbm, query_ref), (token_hbm, token_ref)), sems
    )
    copies[0].wait()
    labels = label_ref[...]
    label_column, slot, slot_column = routed(labels)
    home = home_plane()
    place_ref[...] = one_hot((labels ^ home) * pitch + slot == iota(place_ref.shape, 0))
    back_ref[...] = one_hot((label_column ^ home) * pitch + slot_column == iota(back_ref.shape, 1))
    copies[1].wait()
    pack(cot_ref[0], place_ref, message_refs, pitch)
    for c in copies[2:]:
        c.wait()


def gather_body(order, pitch, *refs):
    *message_refs, rows_ref = refs
    width = message_refs[0].shape[1]
    ordered = [message_refs[order.index(k)] for k in range(len(order))]
    for j, column in enumerate(from_messages(ordered, pitch, rows_ref.shape[0])):
        rows_ref[:, j * width : (j + 1) * width] = column


def combine_body(pitch, *refs):
    partial_refs, message_refs = refs[:SPLIT], refs[SPLIT:]
    total = partial_refs[0][...].astype(F32)
    for partial_ref in partial_refs[1:]:
        total += partial_ref[...].astype(F32)
    to_messages(total.astype(BF16), message_refs, pitch)


def attention_body(
    pitch, query_ref, token_ref, key_ref, value_ref, mask_ref, near_ref, far_ref, place_ref, mixed_ref, *message_refs
):
    rows, features = query_ref.shape[1:]
    width = features // HEADS
    position = lax.axis_index("ep")
    odd = position % 2
    inside = (position > 0) & (position < lax.axis_size("ep") - 1)
    mask_row = 2 * HEADS * HALO
    mask = jnp.concatenate(
        [
            near_ref[mask_row : mask_row + 1, :HALO].astype(F32),
            mask_ref[...].astype(F32),
            far_ref[mask_row : mask_row + 1, :HALO].astype(F32) * jnp.where(inside, 1.0, 0.0),
        ],
        axis=1,
    )
    count = rows + 2 * HALO
    column = iota((rows, count), 1)
    near_first = jnp.where(odd == 1, -HALO, rows)
    far_first = jnp.where(odd == 1, rows, -HALO) - HALO - rows
    first = jnp.where(column < HALO, near_first, jnp.where(column < HALO + rows, -HALO, far_first))
    offset = column + first - iota((rows, count), 0)
    usable = (jnp.abs(offset) <= HALO) & ((mask > 0.5) | (offset == 0))
    factor = width ** (-0.5) * LOG2_E
    scored, valued, weighted = [], [], []
    for head in range(HEADS):
        columns = slice(head * width, (head + 1) * width)
        at, value_at = head * HALO, (HEADS + head) * HALO
        keys = [near_ref[at : at + HALO, :], key_ref[0, :, columns], far_ref[at : at + HALO, :]]
        values = [
            near_ref[value_at : value_at + HALO, :],
            value_ref[0, :, columns],
            far_ref[value_at : value_at + HALO, :],
        ]
        scored.append(dot(query_ref[0, :, columns], jnp.concatenate(keys, axis=0), (1, 1)))
        valued.append(jnp.concatenate(values, axis=0))
    for scores in scored:
        scores = jnp.where(usable, scores, NEG_FILL)
        raised = jnp.exp2((scores - jnp.max(scores, axis=1, keepdims=True)) * factor)
        weighted.append((raised.astype(BF16), 1.0 / jnp.sum(raised, axis=1, keepdims=True)))
    for head, (raised, share) in enumerate(weighted):
        columns = slice(head * width, (head + 1) * width)
        attended = dot(raised, valued[head]) * share
        mixed_ref[:, columns] = (token_ref[0, :, columns].astype(F32) + attended).astype(BF16)
    pack(mixed_ref[...], place_ref, message_refs, pitch)


def far_part(refs, which):
    halves = [r.shape[0] // 2 for r in refs]
    return jnp.concatenate([r[which * n : (which + 1) * n, :] for r, n in zip(refs, halves, strict=True)], axis=0)


def expert_body(*refs):
    *row_refs, in_ref, out_ref, hidden_ref, partial_ref = refs
    rows = row_refs[0][...] if len(row_refs) == 1 else far_part(row_refs, 0)
    for at in range(0, in_ref.shape[1], STEP):
        hidden_ref[:, at : at + STEP] = jax.nn.gelu(dot(rows, in_ref[:, at : at + STEP])).astype(BF16)
    hidden = hidden_ref[...]
    for at in range(0, out_ref.shape[1], STEP):
        partial_ref[:, at : at + STEP] = dot(hidden, out_ref[:, at : at + STEP]).astype(BF16)


def finish_body(order, pitch, mixed_ref, back_ref, *refs):
    *message_refs, layer_ref = refs
    width = message_refs[0].shape[1]
    ordered = [message_refs[order.index(k)] for k in range(len(order))]
    for j, column in enumerate(from_messages(ordered, pitch, back_ref.shape[1])):
        columns = slice(j * width, (j + 1) * width)
        taken = dot(back_ref[...], column)
        layer_ref[0, :, columns] = (mixed_ref[:, columns].astype(F32) + taken).astype(BF16)


def half_terms(refs, side):
    hidden_refs, cot_refs = refs[:SPLIT], refs[SPLIT : 2 * SPLIT - 1]
    cot = jnp.concatenate([c[...] for c in cot_refs] + [far_part(refs[2 * SPLIT - 1 : 2 * SPLIT + 1], 1)], axis=0)
    half = hidden_refs[0].shape[1] // 2
    start = (lax.axis_index("grp") ^ side) * half
    for at in range(0, half, STEP):
        columns = pl.ds(pl.multiple_of(start + at, STEP), STEP)
        hidden = jnp.concatenate([h[:, columns] for h in hidden_refs], axis=0)
        yield at, dot(hidden, cot, (0, 0)).astype(BF16)


def other_half_body(*refs):
    piece_refs = refs[2 * SPLIT + 1 :]
    rows = piece_refs[0].shape[0]
    for at, term in half_terms(refs, 1):
        for r in range(0, STEP, rows):
            piece_refs[(at + r) // rows][...] = term[r : r + rows, :]


def own_half_body(*refs):
    *piece_refs, grad_ref, done_ref = refs[2 * SPLIT + 1 :]
    rows = piece_refs[0].shape[0]
    done_ref[...] = jnp.zeros_like(done_ref)
    for at, term in half_terms(refs, 0):
        for r in range(0, STEP, rows):
            theirs = piece_refs[(at + r) // rows][...].astype(F32)
            grad_ref[0, at + r : at + r + rows, :] = (term[r : r + rows, :].astype(F32) + theirs).astype(BF16)


def whole_term_body(*refs):
    hidden = jnp.concatenate([h[...] for h in refs[:SPLIT]], axis=0)
    cot = jnp.concatenate([c[...] for c in refs[SPLIT : 2 * SPLIT - 1]] + [far_part(refs[-3:-1], 1)], axis=0)
    refs[-1][...] = dot(hidden, cot, (0, 0)).astype(BF16)


def permute(value, apart):
    return lax.ppermute(value, "ep", [(i, i ^ apart) for i in range(lax.axis_size("ep"))])


def forward_body(first_row, rows_ref, cot_ref, both_ref):
    count = both_ref.shape[0] // 2
    both_ref[:count, :] = rows_ref[first_row : first_row + count, :]
    both_ref[count:, :] = cot_ref[first_row : first_row + count, :]


def forwarded(rows, cot, first_row, count, apart):
    (both,) = call(functools.partial(forward_body, first_row), [out(2 * count, rows.shape[1])], vmem=(rows, cot))
    return permute(both, apart)


def of_other_core(value):
    size = lax.axis_size("grp")
    return lax.ppermute(value[:16, :128], "grp", [(i, i ^ 1) for i in range(size)])


def along_line(messages):
    return [m if k == 0 else permute(m, SPLIT * k) for k, m in enumerate(messages)]


def shards(tokens, queries, keys, values, key_mask, labels, cotangent, weight_in, weight_out):
    rows_here, features = tokens.shape[1:]
    axis_count = lax.axis_size("ep")
    experts = axis_count // SPLIT
    capacity = rows_here // experts + max(1, rows_here // (8 * experts))
    width = features // PARTS
    pitch = capacity + capacity % 2
    height = -(-PARTS * pitch // 16) * 16
    plane_rows = -(-experts * pitch // 16) * 16
    hidden_units = weight_in.shape[1]
    head_width = features // HEADS
    label_row = labels.reshape(1, rows_here)
    message = out(height, width)
    block = out(1, rows_here, features)
    row_ints = pltpu.VMEM((1, rows_here), jnp.int32)
    block_scratch = pltpu.VMEM((1, rows_here, features), BF16)

    halo = out(2 * HEADS * HALO + 16, head_width)
    near, far, key_here, value_here, mask_here = call(
        halo_body,
        (halo, halo, block, block, out(1, rows_here, dtype=jnp.int32)),
        hbm=(keys, values, key_mask),
        scratch=[pltpu.SemaphoreType.DMA((3,))],
    )
    near = permute(near, 1)
    steps = [(i, i + 1) for i in range(1, axis_count - 1, 2)]
    far = lax.ppermute(far, "ep", steps + [(j, i) for i, j in steps])

    place, place_back, query_here, token_here, *sent = call(
        functools.partial(pack_body, pitch),
        [out(plane_rows, rows_here), out(rows_here, plane_rows), block, block]
        + [message] * experts,
        hbm=(cotangent, label_row, queries, tokens),
        after=(key_here,),
        scratch=[block_scratch, row_ints, pltpu.SemaphoreType.DMA((4,))],
        size=0,
    )
    cot_got = along_line(sent)
    in_here, out_here = weight_in, weight_out.reshape(weight_out.shape[1:])

    mixed, *sent = call(
        functools.partial(attention_body, pitch),
        [out(rows_here, features)] + [message] * experts,
        vmem=(query_here, token_here, key_here, value_here, mask_here, near, far, place),
        flops=4 * rows_here * (rows_here + 2 * HALO) * features,
    )

    order = [0, 2, 1, *range(3, experts)]
    (cot_rows,) = call(
        functools.partial(gather_body, order, pitch),
        [out(plane_rows, features)],
        vmem=[cot_got[k] for k in order],
        after=(mixed,),
        size=0,
    )
    cot_x, cot_y = permute(cot_rows, 1), permute(cot_rows, 2)
    (rows,) = call(
        functools.partial(gather_body, range(experts), pitch), [out(plane_rows, features)], vmem=along_line(sent)
    )

    row_x, row_y = permute(rows, 1), permute(rows, 2)
    part = plane_rows // 32 * 16
    far = (forwarded(row_x, cot_x, 0, part, 2), forwarded(row_y, cot_y, part, plane_rows - part, 1))
    hiddens, partials = [], []
    for pieces, first in (((rows,), (cot_x, cot_y)), ((row_x,), ()), ((row_y,), ()), (far, ())):
        hidden, partial = call(
            expert_body,
            [out(plane_rows, hidden_units), out(plane_rows, features)],
            vmem=(*pieces, in_here, out_here),
            after=(*first, *hiddens[:1], *[of_other_core(h) for h in hiddens[:1] if len(hiddens) > 2]),
            flops=4 * plane_rows * features * hidden_units,
        )
        hiddens.append(hidden)
        partials.append(partial)

    sums = [p if k == 0 else permute(p, k) for k, p in enumerate(partials)]

    inputs = (*hiddens, cot_rows, cot_x, cot_y, *far)
    flops = SPLIT * plane_rows * features * hidden_units
    if lax.axis_size("grp") == 2:
        half = hidden_units // 2
        pieces = call(
            other_half_body, [out(half // PIECES, features)] * PIECES, vmem=inputs, after=sums[1:3], flops=flops
        )
        theirs = [lax.ppermute(piece, "grp", [(0, 1), (1, 0)]) for piece in pieces]
        grad, done = call(
            own_half_body,
            [out(1, half, features), out(8, 128, dtype=F32)],
            vmem=(*inputs, *theirs),
            flops=flops,
        )
        ready = (done,)
    else:
        (term,) = call(whole_term_body, [out(hidden_units, features)], vmem=inputs, flops=2 * flops)
        grad = lax.psum_scatter(term, "grp", scatter_dimension=0, tiled=True)[None]
        ready = ()
    sent = call(functools.partial(combine_body, pitch), [message] * experts, vmem=sums)
    back = along_line(sent)
    order = [0, *range(experts - 1, 0, -1)]
    (layer_out,) = call(
        functools.partial(finish_body, order, pitch), [block], vmem=(mixed, place_back, *[back[k] for k in order]), after=ready
    )
    return (layer_out, grad)


def solution(mesh):
    in_specs = (
        P("grp", "ep", None),
        P("grp", "ep", None),
        P("grp", "ep", None),
        P("grp", "ep", None),
        P("grp", "ep"),
        P("grp", "ep", None),
        P("grp", "ep", None),
        P(None, "ep"),
        P("ep", None, None),
    )
    out_specs = (P("grp", "ep", None), P("ep", "grp", None))
    return jax.shard_map(shards, mesh=mesh, in_specs=in_specs, out_specs=out_specs, check_vma=False)
```
